32 devices in a mesh: rows: 8 (over z, x), cols: 4 (over y, core).
Axes of the slice: x: 2, y: 2, z: 4, core: 2. Of those that a mesh axis runs over, the one named last changes fastest.
Arguments:
- conc: float32 [8, 48, 64, 512], P(None, None, 'rows', 'cols'), may hold values from 0 to 2
- nwp: bfloat16 [2, 137, 16384], P(None, None, 'rows'), may hold values from -0.3 to 0.3
- lev_lo: int32 [48], replicated, may hold values from 0 to 135
- frac: float32 [48], replicated, may hold values from 0 to 1
- pick: int32 [8, 4, 8, 64], P('rows', 'cols'), may hold values from 0 to 2047
- corner_slot: int32 [4, 64, 512], P(None, 'rows', 'cols'), may hold values from 0 to 511
- corner_wt: float32 [4, 64, 512], P(None, 'rows', 'cols'), may hold values from 0.25 to 1
- settle: float32 [8], replicated, may hold values from 0.015 to 0.15
- source_mask: int32 [64, 512], P('rows', 'cols'), may hold values 0 or 1
- profile: float32 [8, 48], replicated, may hold values from 0.1 to 1
Outputs:
- final_conc: float32 [8, 48, 64, 512], P(None, None, 'rows', 'cols')
- deposit: float32 [8, 64, 512], P(None, 'rows', 'cols')
The draws below stay inside these ranges and needn't reach their ends.
All inputs are finite; a program needn't handle non-finite values. No bound on the sum of `source_mask` on one device may be relied on, other than what follows from the above.
Results may differ from the reference program's by a relative error of at most 0.0013.
Values may be sent and summed in bfloat16 or wider, within the bound.
A program may use at most 128 MiB of HBM per device.

```python
import math
import jax
import jax.numpy as jnp

BINS = 8
ZL = 48
LN = 137
RD = 8
CD = 128
NC_DEV = 2048
CAP = 64
STEPS = 3
SLOTS = 512
NY = 64
NX = 512
NWP_COLS = 16384
N_ROWS = 8
N_COLS = 4


def draw_conc(key, part):
    shape = (BINS, ZL, NY, NX)
    pick_key = jax.random.fold_in(key, 11)
    high_key = jax.random.fold_in(key, 12)
    low_key = jax.random.fold_in(key, 13)
    heavy = jax.random.bernoulli(pick_key, 0.5, shape)
    high_part = jax.random.uniform(high_key, shape, jnp.float32)
    low_part = jax.random.uniform(low_key, shape, jnp.float32)
    values = jnp.where(heavy, 1.5 + 0.5 * high_part, 0.5 * low_part)
    return values.astype(jnp.float32)


def draw_nwp(key, part):
    shape = (2, LN, NWP_COLS)
    base = jax.random.uniform(jax.random.fold_in(key, 21), shape, jnp.float32, -1.0, 1.0)
    values = 0.29 * base
    return values.astype(jnp.bfloat16)


def place_ends(result, own_key, least, high):
    shape = result.shape
    index_at = [jax.random.randint(jax.random.fold_in(own_key, axis), (), 0, shape[axis]) for axis in range(len(shape))]
    result = result.at[tuple(index_at)].set(least)
    longest = shape.index(max(shape))
    index_at[longest] = (index_at[longest] + 1) % shape[longest]
    return result.at[tuple(index_at)].set(high)


def shard_levels(key, dims, shards, least, largest):
    def one(dim, blocks):
        steps = jax.random.uniform(jax.random.fold_in(jax.random.fold_in(key, 6), dim), (blocks,), jnp.float32, least / len(shards), largest / len(shards))
        return jnp.repeat(jnp.exp(steps), dims[dim] // blocks).reshape((-1,) + (1,) * (len(dims) - dim - 1))

    factor_of = one(*shards[0])
    for cut in shards[1:]:
        factor_of = factor_of * one(*cut)
    return factor_of


def setup_inputs(seed: int = 0) -> dict:
    arg_keys = jax.random.split(jax.random.key(seed), 11)
    conc = draw_conc(jax.random.fold_in(arg_keys[10], 71), 0)
    nwp = draw_nwp(jax.random.fold_in(arg_keys[10], 71), 0)
    lev_lo = place_ends(jax.random.randint(arg_keys[2], (ZL,), 0, LN - 1), jax.random.fold_in(arg_keys[2], 1), 0, (LN - 1) - 1).astype(jnp.int32)
    frac = jnp.clip(jax.random.uniform(arg_keys[3], (ZL,), jnp.float32, 0.0, 1.0), 0.0, 1.0)
    pick = place_ends(jax.random.randint(arg_keys[4], (N_ROWS, N_COLS, N_ROWS, CAP), 0, NC_DEV), jax.random.fold_in(arg_keys[4], 1), 0, NC_DEV - 1).astype(jnp.int32)
    corner_slot = place_ends(jax.random.randint(arg_keys[5], (4, NY, NX), 0, SLOTS), jax.random.fold_in(arg_keys[5], 1), 0, SLOTS - 1).astype(jnp.int32)
    corner_wt = jnp.clip(jnp.exp(math.log(1.0) - 1.3862944 * jax.random.uniform(arg_keys[6], (4, NY, NX), jnp.float32) ** shard_levels(arg_keys[6], (4, NY, NX), ((1, 8), (2, 4)), -0.2, 0.2)), 0.25, 1.0)
    settle = jnp.clip(jnp.exp(jax.random.uniform(arg_keys[7], (BINS,), jnp.float32, math.log(0.015), math.log(0.15))), 0.015, 0.15)
    source_mask = place_ends((jax.random.randint(arg_keys[8], (NY, NX), 0, 16) < 1).astype(jnp.int32), jax.random.fold_in(arg_keys[8], 1), 0, 1)
    profile = jnp.clip(jnp.exp(jax.random.uniform(arg_keys[9], (BINS, ZL), jnp.float32, math.log(0.1), math.log(1.0))), 0.1, 1.0)
    return dict(conc=conc, nwp=nwp, lev_lo=lev_lo, frac=frac, pick=pick, corner_slot=corner_slot, corner_wt=corner_wt, settle=settle, source_mask=source_mask, profile=profile)


KAPPA = 0.05


def vertical(columns, lev_lo, frac):
    lower = jnp.take(columns, lev_lo, axis=1).astype(jnp.float32)
    upper = jnp.take(columns, lev_lo + 1, axis=1).astype(jnp.float32)
    share = frac[None, :, None]
    return ((1.0 - share) * lower + share * upper).astype(jnp.bfloat16)


def horizontal(levels, slots, corner_wt):
    weight_sum = jnp.sum(corner_wt, axis=0)
    norm_wt = corner_wt / weight_sum
    winds = None
    for corner in range(4):
        values = jnp.take(levels, slots[corner], axis=2).astype(jnp.float32)
        term = norm_wt[corner] * values
        winds = term if winds is None else winds + term
    return winds


def advance(padded, winds, emission, settle):
    east = 0.5 * (winds[0][:, :, 1:] + winds[0][:, :, :-1])
    north = 0.5 * (winds[1][:, 1:, :] + winds[1][:, :-1, :])
    flux_x = jnp.maximum(east, 0.0) * padded[..., :, :-1] + jnp.minimum(east, 0.0) * padded[..., :, 1:]
    flux_y = jnp.maximum(north, 0.0) * padded[..., :-1, :] + jnp.minimum(north, 0.0) * padded[..., 1:, :]
    div_x = (flux_x[..., 1:] - flux_x[..., :-1])[..., 1:-1, :]
    div_y = (flux_y[..., 1:, :] - flux_y[..., :-1, :])[..., :, 1:-1]
    centre = padded[..., 1:-1, 1:-1]
    lap = padded[..., 2:, 1:-1] + padded[..., :-2, 1:-1] + padded[..., 1:-1, 2:] + padded[..., 1:-1, :-2] - 4.0 * centre
    falling = settle[:, None, None, None] * centre
    arriving = jnp.concatenate([jnp.zeros_like(falling[:, :1]), falling[:, :-1]], axis=1)
    fresh = centre - div_x - div_y + KAPPA * lap - falling + arriving + emission
    return fresh, falling[:, -1]


def reference(conc, nwp, lev_lo, frac, pick, corner_slot, corner_wt, settle, source_mask, profile):
    levels = vertical(nwp, lev_lo, frac)
    based = pick + (jnp.arange(N_ROWS, dtype=jnp.int32) * NC_DEV)[:, None, None, None]
    table = jnp.transpose(based, (2, 1, 0, 3)).reshape(N_ROWS, N_COLS, SLOTS)
    row_of = jnp.arange(NY, dtype=jnp.int32) // RD
    col_of = jnp.arange(NX, dtype=jnp.int32) // CD
    sources = table[row_of[None, :, None], col_of[None, None, :], corner_slot]
    winds = horizontal(levels, sources, corner_wt)
    emission = source_mask.astype(jnp.float32)[None, None] * profile[:, :, None, None]
    widths = ((0, 0), (0, 0), (1, 1), (1, 1))
    wind_pad = jnp.pad(winds, widths)
    state = conc
    deposit = jnp.zeros((BINS, NY, NX), jnp.float32)
    for step in range(STEPS):
        state, fallen = advance(jnp.pad(state, widths), wind_pad, emission, settle)
        deposit = deposit + fallen
    return state, deposit
```

```python
import functools

import jax
import jax.numpy as jnp
from jax import lax
from jax.experimental import pallas as pl
from jax.experimental.pallas import tpu as pltpu
from jax.sharding import PartitionSpec as P

STEPS = 3
KAPPA = 0.05
MESH = pl.DeviceIdType.MESH
UP, DOWN, LEFT, RIGHT = range(4)
BF16 = jnp.bfloat16
F32 = jnp.float32


def kernel(
    n_rows,
    n_cols,
    conc,
    nwp,
    lev_lo,
    frac,
    pick,
    corner_slot,
    corner_wt,
    settle,
    source_mask,
    profile,
    out,
    deposit,
    levels,
    onehot,
    sent,
    got,
    turned,
    norm_wt,
    table_hi,
    table_lo,
    winds,
    wind_row_out,
    wind_row_in,
    wind_col_out,
    wind_col_in,
    row_out,
    row_in,
    col_out,
    col_in,
    edge,
    coef,
    state,
    band_send,
    band_recv,
    wind_send,
    wind_recv,
    halo_send,
    halo_recv,
):
    bins, nz, rd, cd = conc.shape
    ln, columns = nwp.shape[1:]
    cap = pick.shape[3]
    slots = n_rows * cap
    r = lax.axis_index("rows")
    c = lax.axis_index("cols")
    has = (r > 0, r < n_rows - 1, c > 0, c < n_cols - 1)
    target = ({"rows": r - 1}, {"rows": r + 1}, {"cols": c - 1}, {"cols": c + 1})
    lane = lax.broadcasted_iota(jnp.int32, (rd, cd), 1)
    sub = lax.broadcasted_iota(jnp.int32, (rd, cd), 0)
    odd = (lane % 2) == 1
    first_lane, last_lane = lane == 0, lane == cd - 1
    first_sub, last_sub = sub == 0, sub == rd - 1

    barrier = pltpu.get_barrier_semaphore()
    for d in range(1, n_rows):
        pl.semaphore_signal(
            barrier, inc=1, device_id={"rows": lax.rem(r + d, n_rows)}, device_id_type=MESH
        )
    for side in (LEFT, RIGHT):

        @pl.when(has[side])
        def _():
            pl.semaphore_signal(barrier, inc=1, device_id=target[side], device_id_type=MESH)

    for side in (UP, DOWN):

        @pl.when(jnp.logical_not(has[side]))
        def _():
            row_in[:, side] = jnp.zeros(row_in.shape[:1] + row_in.shape[2:], BF16)
            wind_row_in[side] = jnp.zeros(wind_row_in.shape[1:], BF16)

    for side in (LEFT, RIGHT):

        @pl.when(jnp.logical_not(has[side]))
        def _():
            col_in[:, side - 2] = jnp.zeros(col_in.shape[:1] + col_in.shape[2:], F32)
            wind_col_in[side - 2] = jnp.zeros(wind_col_in.shape[1:], F32)

    def pack_group(planes, g):
        acc = jnp.zeros((rd, cd), F32)
        for j, plane in enumerate(planes):
            here = (lane == 2 * j) | (lane == 2 * j + 1)
            acc = jnp.where(here, pltpu.roll(plane, 2 * j + 1, 1), acc)
        return pltpu.roll(acc, 16 * g, 1)

    def unpack(left, right):
        return jnp.where(odd, pltpu.roll(left, 1, 1), pltpu.roll(right, cd - 1, 1))

    def halo_copy(stage, side, b):
        other = side ^ 1
        if side < 2:
            src, dst = row_out.at[stage, side, b], row_in.at[stage, other, b]
        else:
            src, dst = col_out.at[stage, b], col_in.at[stage, other - 2, b]
        return pltpu.make_async_remote_copy(
            src_ref=src,
            dst_ref=dst,
            send_sem=halo_send.at[stage, side, b],
            recv_sem=halo_recv.at[stage, other, b],
            device_id=target[side],
            device_id_type=MESH,
        )

    def halo_arrival(stage, side, b):
        if side < 2:
            src, dst = row_out.at[stage, side, b], row_in.at[stage, side, b]
        else:
            src, dst = col_out.at[stage, b], col_in.at[stage, side - 2, b]
        return pltpu.make_async_remote_copy(
            src_ref=src,
            dst_ref=dst,
            send_sem=halo_send.at[stage, side, b],
            recv_sem=halo_recv.at[stage, side, b],
            device_id=target[side],
            device_id_type=MESH,
        )

    def wind_copy(side):
        other = side ^ 1
        if side < 2:
            src, dst = wind_row_out.at[side], wind_row_in.at[other]
        else:
            src, dst = wind_col_out, wind_col_in.at[other - 2]
        return pltpu.make_async_remote_copy(
            src_ref=src,
            dst_ref=dst,
            send_sem=wind_send.at[side],
            recv_sem=wind_recv.at[other],
            device_id=target[side],
            device_id_type=MESH,
        )

    def wind_arrival(side):
        if side < 2:
            src, dst = wind_row_out.at[side], wind_row_in.at[side]
        else:
            src, dst = wind_col_out, wind_col_in.at[side - 2]
        return pltpu.make_async_remote_copy(
            src_ref=src,
            dst_ref=dst,
            send_sem=wind_send.at[side],
            recv_sem=wind_recv.at[side],
            device_id=target[side],
            device_id_type=MESH,
        )

    def pack_rows(ref, stage, b):
        flat = ref.reshape(bins * nz * rd, cd)
        base = b * (nz * rd)
        row_out[stage, UP, b] = flat[pl.ds(base, nz, stride=rd), :].astype(BF16)
        row_out[stage, DOWN, b] = flat[pl.ds(base + rd - 1, nz, stride=rd), :].astype(BF16)

    def send_halo(stage, b):
        for side in range(4):

            @pl.when(has[side])
            def _():
                halo_copy(stage, side, b).start()

    def first_pack(b, _):
        def group(g, acc):
            return acc + pack_group([conc[b, g * 8 + j] for j in range(8)], g)

        col_out[0, b] = lax.fori_loop(0, nz // 8, group, jnp.zeros((rd, cd), F32))
        pack_rows(conc, 0, b)
        return 0

    lax.fori_loop(0, bins, first_pack, 0)

    pl.semaphore_wait(
        barrier, n_rows - 1 + has[LEFT].astype(jnp.int32) + has[RIGHT].astype(jnp.int32)
    )

    def first_send(b, _):
        send_halo(0, b)
        return 0

    lax.fori_loop(0, bins, first_send, 0)

    diag = lax.broadcasted_iota(jnp.int32, (nz, nz), 0) == lax.broadcasted_iota(
        jnp.int32, (nz, nz), 1
    )
    low = jnp.sum(
        jnp.where(diag, lev_lo[...].astype(F32), 0.0), axis=1, keepdims=True
    ).astype(jnp.int32)
    share = jnp.sum(jnp.where(diag, frac[...], 0.0), axis=1, keepdims=True)
    level_id = lax.broadcasted_iota(jnp.int32, (nz, ln), 1)
    interp = jnp.where(level_id == low, 1.0 - share, 0.0) + jnp.where(
        level_id == low + 1, share, 0.0
    )
    interp_hi = interp.astype(BF16)
    rest = interp - interp_hi.astype(F32)
    interp_mid = rest.astype(BF16)
    interp_lo = (rest - interp_mid.astype(F32)).astype(BF16)
    parts = jnp.concatenate([interp_hi, interp_mid, interp_lo], axis=0)
    for f in range(2):
        mixed = jnp.dot(parts, nwp[f], preferred_element_type=F32)
        levels[f * nz : (f + 1) * nz, :] = (
            mixed[:nz] + mixed[nz : 2 * nz] + mixed[2 * nz :]
        ).astype(BF16)

    def band_copy(source, dest, d):
        return pltpu.make_async_remote_copy(
            src_ref=sent.at[pl.ds(pl.multiple_of(dest * cap, cap), cap)],
            dst_ref=got.at[pl.ds(pl.multiple_of(source * cap, cap), cap)],
            send_sem=band_send.at[d],
            recv_sem=band_recv.at[d],
            device_id={"rows": dest},
            device_id_type=MESH,
        )

    per = 4
    width = per * cap

    def choose(p, _):
        wanted = jnp.concatenate([pick[0, 0, pl.ds(p * per + i, 1), :] for i in range(per)], axis=1)
        step = 128

        def fill(t, _):
            ids = lax.broadcasted_iota(jnp.int32, (step, width), 0) + t * step
            onehot[pl.ds(t * step, step), :] = jnp.where(ids == wanted, 1.0, 0.0).astype(BF16)
            return 0

        lax.fori_loop(0, columns // step, fill, 0)
        chosen = jnp.dot(levels[...], onehot[...], preferred_element_type=F32)
        chosen = jnp.concatenate([chosen, jnp.zeros((128 - 2 * nz, width), F32)], axis=0)
        sent[pl.ds(p * width, width), :] = chosen.T.astype(BF16)
        return 0

    lax.fori_loop(0, n_rows // per, choose, 0)
    for d in range(1, n_rows):
        band_copy(r, lax.rem(r + d, n_rows), d).start()

    weights = corner_wt[...]
    norm_wt[...] = weights / (weights[0] + weights[1] + weights[2] + weights[3])
    chunk = 128

    def fill_table(i, _):
        p = i // (slots // chunk)
        t = i % (slots // chunk)
        ids = lax.broadcasted_iota(jnp.int32, (chunk, cd), 0) + t * chunk
        for half in range(2):
            total = jnp.zeros((chunk, cd), F32)
            for q in range(4):
                slot = corner_slot[q, pl.ds(2 * p + half, 1), :]
                wt = norm_wt[q, pl.ds(2 * p + half, 1), :]
                total = total + jnp.where(ids == slot, wt, 0.0)
            hi = total.astype(BF16)
            where = (p, pl.ds(t * chunk, chunk), pl.ds(half * cd, cd))
            table_hi[where] = hi
            table_lo[where] = (total - hi.astype(F32)).astype(BF16)
        return 0

    lax.fori_loop(0, (rd // 2) * (slots // chunk), fill_table, 0)

    own = pl.ds(pl.multiple_of(r * cap, cap), cap)
    got[own, :] = sent[own, :]
    for d in range(1, n_rows):
        band_copy(lax.rem(r + n_rows - d, n_rows), r, d).wait_recv()
    for t in range(slots // 128):
        turned[:, t * 128 : (t + 1) * 128] = (
            got[t * 128 : (t + 1) * 128, :].astype(F32).T.astype(BF16)
        )
    flat_winds = winds.reshape(2 * nz * rd, cd)
    for p in range(rd // 2):
        blown = jnp.dot(turned[...], table_hi[p], preferred_element_type=F32) + jnp.dot(
            turned[...], table_lo[p], preferred_element_type=F32
        )
        flat_winds[pl.ds(2 * p, 2 * nz, stride=rd), :] = blown[: 2 * nz, :cd]
        flat_winds[pl.ds(2 * p + 1, 2 * nz, stride=rd), :] = blown[: 2 * nz, cd:]

    wind_row_out[UP] = flat_winds[pl.ds(nz * rd, nz, stride=rd), :].astype(BF16)
    wind_row_out[DOWN] = flat_winds[pl.ds(nz * rd + rd - 1, nz, stride=rd), :].astype(BF16)

    def wind_group(g, acc):
        return acc + pack_group([winds[g * 8 + j] for j in range(8)], g)

    wind_col_out[...] = lax.fori_loop(0, nz // 8, wind_group, jnp.zeros((rd, cd), F32))
    for side in range(4):

        @pl.when(has[side])
        def _():
            wind_copy(side).start()

    for side in range(4):

        @pl.when(has[side])
        def _():
            wind_arrival(side).wait_recv()

    def spread_rows(up, down):
        flat = edge.reshape(nz * rd, cd)
        flat[pl.ds(0, nz, stride=rd), :] = up.astype(F32)
        flat[pl.ds(rd - 1, nz, stride=rd), :] = down.astype(F32)

    def across(plane, rim):
        ahead = jnp.where(last_lane, rim, pltpu.roll(plane, cd - 1, 1))
        behind = jnp.where(first_lane, rim, pltpu.roll(plane, 1, 1))
        return ahead, behind

    def along(plane, rim):
        below = jnp.where(last_sub, rim, pltpu.roll(plane, rd - 1, 0))
        above = jnp.where(first_sub, rim, pltpu.roll(plane, 1, 0))
        return below, above

    edge[...] = jnp.zeros_like(edge)
    spread_rows(wind_row_in[UP], wind_row_in[DOWN])
    wind_rim = unpack(wind_col_in[0], wind_col_in[1])

    def coefficients(g, _):
        rims = pltpu.roll(wind_rim, lax.rem(cd - 16 * g, cd), 1)
        for j in range(8):
            k = g * 8 + j
            u, v = winds[k], winds[nz + k]
            u_ahead, u_behind = across(u, pltpu.roll(rims, cd - 2 * j - 1, 1))
            v_below, v_above = along(v, edge[k])
            right, left = 0.5 * (u + u_ahead), 0.5 * (u + u_behind)
            down, up = 0.5 * (v + v_below), 0.5 * (v + v_above)
            coef[0, k] = (
                (1.0 - 4.0 * KAPPA)
                - jnp.maximum(right, 0.0)
                + jnp.minimum(left, 0.0)
                - jnp.maximum(down, 0.0)
                + jnp.minimum(up, 0.0)
            )
            coef[1, k] = KAPPA - jnp.minimum(right, 0.0)
            coef[2, k] = KAPPA + jnp.maximum(left, 0.0)
            coef[3, k] = KAPPA - jnp.minimum(down, 0.0)
            coef[4, k] = KAPPA + jnp.maximum(up, 0.0)
        return 0

    lax.fori_loop(0, nz // 8, coefficients, 0)

    flag = source_mask[...].astype(F32)
    for stage in range(STEPS):
        src = conc if stage == 0 else state
        dst = out if stage == STEPS - 1 else state
        last = stage == STEPS - 1

        def one_bin(b, _):
            for side in range(4):

                @pl.when(has[side])
                def _():
                    halo_arrival(stage, side, b).wait_recv()

            spread_rows(row_in[stage, UP, b], row_in[stage, DOWN, b])
            rim = unpack(col_in[stage, 0, b], col_in[stage, 1, b])
            sink = settle[b]

            def group(g, carry):
                arriving, packed = carry
                rims = pltpu.roll(rim, lax.rem(cd - 16 * g, cd), 1)
                fresh = []
                for j in range(8):
                    k = g * 8 + j
                    a = src[b, k]
                    ahead, behind = across(a, pltpu.roll(rims, cd - 2 * j - 1, 1))
                    below, above = along(a, edge[k])
                    falling = sink * a
                    new = (
                        (coef[0, k] * a + coef[1, k] * ahead)
                        + (coef[2, k] * behind + coef[3, k] * below)
                        + (coef[4, k] * above + flag * profile[b, k])
                        + (arriving - falling)
                    )
                    dst[b, k] = new
                    fresh.append(new)
                    arriving = falling
                if not last:
                    packed = packed + pack_group(fresh, g)
                return arriving, packed

            zero = jnp.zeros((rd, cd), F32)
            fallen, packed = lax.fori_loop(0, nz // 8, group, (zero, zero))
            deposit[b] = fallen if stage == 0 else deposit[b] + fallen
            if not last:
                col_out[stage + 1, b] = packed
                pack_rows(dst, stage + 1, b)
                send_halo(stage + 1, b)
            return 0

        lax.fori_loop(0, bins, one_bin, 0)

    for d in range(1, n_rows):
        band_copy(r, lax.rem(r + d, n_rows), d).wait_send()
    for side in range(4):

        @pl.when(has[side])
        def _():
            wind_copy(side).wait_send()

            def drain(b, _):
                for stage in range(STEPS):
                    halo_copy(stage, side, b).wait_send()
                return 0

            lax.fori_loop(0, bins, drain, 0)


def per_device(conc, nwp, lev_lo, frac, pick, corner_slot, corner_wt, settle, source_mask, profile):
    n_rows, n_cols = lax.axis_size("rows"), lax.axis_size("cols")
    bins, nz, rd, cd = conc.shape
    cap = pick.shape[3]
    slots = n_rows * cap
    columns = nwp.shape[2]
    vmem = pl.BlockSpec(memory_space=pltpu.VMEM)
    smem = pl.BlockSpec(memory_space=pltpu.SMEM)
    return pl.pallas_call(
        functools.partial(kernel, n_rows, n_cols),
        out_shape=(
            jax.ShapeDtypeStruct(conc.shape, F32),
            jax.ShapeDtypeStruct((bins, rd, cd), F32),
        ),
        in_specs=[vmem] * 7 + [smem, vmem, smem],
        out_specs=(vmem, vmem),
        scratch_shapes=[
            pltpu.VMEM((2 * nz, columns), BF16),
            pltpu.VMEM((columns, 4 * cap), BF16),
            pltpu.VMEM((slots, 128), BF16),
            pltpu.VMEM((slots, 128), BF16),
            pltpu.VMEM((128, slots), BF16),
            pltpu.VMEM(corner_wt.shape, F32),
            pltpu.VMEM((rd // 2, slots, 2 * cd), BF16),
            pltpu.VMEM((rd // 2, slots, 2 * cd), BF16),
            pltpu.VMEM((2 * nz, rd, cd), F32),
            pltpu.VMEM((2, nz, cd), BF16),
            pltpu.VMEM((2, nz, cd), BF16),
            pltpu.VMEM((rd, cd), F32),
            pltpu.VMEM((2, rd, cd), F32),
            pltpu.VMEM((STEPS, 2, bins, nz, cd), BF16),
            pltpu.VMEM((STEPS, 2, bins, nz, cd), BF16),
            pltpu.VMEM((STEPS, bins, rd, cd), F32),
            pltpu.VMEM((STEPS, 2, bins, rd, cd), F32),
            pltpu.VMEM((nz, rd, cd), F32),
            pltpu.VMEM((5, nz, rd, cd), F32),
            pltpu.VMEM(conc.shape, F32),
            pltpu.SemaphoreType.DMA((n_rows,)),
            pltpu.SemaphoreType.DMA((n_rows,)),
            pltpu.SemaphoreType.DMA((4,)),
            pltpu.SemaphoreType.DMA((4,)),
            pltpu.SemaphoreType.DMA((STEPS, 4, bins)),
            pltpu.SemaphoreType.DMA((STEPS, 4, bins)),
        ],
        compiler_params=pltpu.CompilerParams(
            collective_id=0, has_side_effects=True, vmem_limit_bytes=48 * 1024 * 1024
        ),
        cost_estimate=pl.CostEstimate(
            flops=10**9, bytes_accessed=6 * 10**6, transcendentals=0
        ),
        name="ash",
    )(
        conc,
        nwp,
        lev_lo.reshape(1, -1),
        frac.reshape(1, -1),
        pick,
        corner_slot,
        corner_wt,
        settle,
        source_mask,
        profile,
    )


def solution(mesh):
    placed = (
        P(None, None, "rows", "cols"),
        P(None, None, "rows"),
        P(),
        P(),
        P("rows", "cols", None, None),
        P(None, "rows", "cols"),
        P(None, "rows", "cols"),
        P(),
        P("rows", "cols"),
        P(),
    )
    return jax.shard_map(
        per_device,
        mesh=mesh,
        in_specs=placed,
        out_specs=(P(None, None, "rows", "cols"), P(None, "rows", "cols")),
        check_vma=False,
    )
```

```python
import functools

import jax
import jax.numpy as jnp
from jax import lax
from jax.experimental import pallas as pl
from jax.experimental.pallas import tpu as pltpu
from jax.sharding import PartitionSpec as P

STEPS = 3
KAPPA = 0.05
MESH = pl.DeviceIdType.MESH
UP, DOWN, LEFT, RIGHT = range(4)
BF16 = jnp.bfloat16
F32 = jnp.float32


def kernel(
    n_rows,
    n_cols,
    conc,
    nwp,
    lev_lo,
    frac,
    pick,
    corner_slot,
    corner_wt,
    settle,
    source_mask,
    profile,
    out,
    deposit,
    levels,
    onehot,
    sent,
    got,
    turned,
    norm_wt,
    table_hi,
    table_lo,
    winds,
    wind_row_out,
    wind_row_in,
    wind_col_out,
    wind_col_in,
    row_out,
    row_in,
    col_out,
    col_in,
    coef,
    state_a,
    state_b,
    spread,
    flags,
    band_send,
    band_recv,
    wind_send,
    wind_recv,
    halo_send,
    halo_recv,
):
    bins, nz, rd, cd = conc.shape
    ln, columns = nwp.shape[1:]
    cap = pick.shape[3]
    slots = n_rows * cap
    r = lax.axis_index("rows")
    c = lax.axis_index("cols")
    has = (r > 0, r < n_rows - 1, c > 0, c < n_cols - 1)
    target = ({"rows": r - 1}, {"rows": r + 1}, {"cols": c - 1}, {"cols": c + 1})
    lane = lax.broadcasted_iota(jnp.int32, (rd, cd), 1)
    sub = lax.broadcasted_iota(jnp.int32, (rd, cd), 0)
    odd = (lane % 2) == 1
    first_lane, last_lane = lane == 0, lane == cd - 1
    first_sub, last_sub = sub == 0, sub == rd - 1

    barrier = pltpu.get_barrier_semaphore()
    for d in range(1, n_rows):
        pl.semaphore_signal(
            barrier, inc=1, device_id={"rows": lax.rem(r + d, n_rows)}, device_id_type=MESH
        )
    for side in (LEFT, RIGHT):

        @pl.when(has[side])
        def _():
            pl.semaphore_signal(barrier, inc=1, device_id=target[side], device_id_type=MESH)

    for side in (UP, DOWN):

        @pl.when(jnp.logical_not(has[side]))
        def _():
            row_in[:, side] = jnp.zeros(row_in.shape[:1] + row_in.shape[2:], BF16)
            wind_row_in[side] = jnp.zeros(wind_row_in.shape[1:], BF16)

    for side in (LEFT, RIGHT):

        @pl.when(jnp.logical_not(has[side]))
        def _():
            col_in[:, side - 2] = jnp.zeros(col_in.shape[:1] + col_in.shape[2:], F32)
            wind_col_in[side - 2] = jnp.zeros(wind_col_in.shape[1:], F32)

    groups = nz // rd
    here = [(lane // 2) == g for g in range(groups)]

    def block(g):
        return slice(g * rd, (g + 1) * rd)

    def pack(rows):
        packed = jnp.zeros((rd, cd), F32)
        for y in range(rd):
            acc = jnp.zeros((rd, cd), F32)
            for g in range(groups):
                acc = jnp.where(here[g], pltpu.roll(rows[y][g], 2 * g + 1, 1), acc)
            packed = packed + (pltpu.roll(acc, 2 * groups * y, 1) if y else acc)
        return packed

    def unpack(left, right):
        return jnp.where(odd, pltpu.roll(left, 1, 1), pltpu.roll(right, cd - 1, 1))

    def halo_copy(stage, side, b):
        other = side ^ 1
        if side < 2:
            src, dst = row_out.at[stage, side, b], row_in.at[stage, other, b]
        else:
            src, dst = col_out.at[stage, b], col_in.at[stage, other - 2, b]
        return pltpu.make_async_remote_copy(
            src_ref=src,
            dst_ref=dst,
            send_sem=halo_send.at[stage, side, b],
            recv_sem=halo_recv.at[stage, other, b],
            device_id=target[side],
            device_id_type=MESH,
        )

    def halo_arrival(stage, side, b):
        if side < 2:
            src, dst = row_out.at[stage, side, b], row_in.at[stage, side, b]
        else:
            src, dst = col_out.at[stage, b], col_in.at[stage, side - 2, b]
        return pltpu.make_async_remote_copy(
            src_ref=src,
            dst_ref=dst,
            send_sem=halo_send.at[stage, side, b],
            recv_sem=halo_recv.at[stage, side, b],
            device_id=target[side],
            device_id_type=MESH,
        )

    def wind_copy(side):
        other = side ^ 1
        if side < 2:
            src, dst = wind_row_out.at[side], wind_row_in.at[other]
        else:
            src, dst = wind_col_out, wind_col_in.at[other - 2]
        return pltpu.make_async_remote_copy(
            src_ref=src,
            dst_ref=dst,
            send_sem=wind_send.at[side],
            recv_sem=wind_recv.at[other],
            device_id=target[side],
            device_id_type=MESH,
        )

    def wind_arrival(side):
        if side < 2:
            src, dst = wind_row_out.at[side], wind_row_in.at[side]
        else:
            src, dst = wind_col_out, wind_col_in.at[side - 2]
        return pltpu.make_async_remote_copy(
            src_ref=src,
            dst_ref=dst,
            send_sem=wind_send.at[side],
            recv_sem=wind_recv.at[side],
            device_id=target[side],
            device_id_type=MESH,
        )

    def send_halo(stage, b):
        for side in range(4):

            @pl.when(has[side])
            def _():
                halo_copy(stage, side, b).start()

    flat_conc = conc.reshape(bins * nz * rd, cd)

    def first_pack(b, _):
        rows = []
        for y in range(rd):
            row = flat_conc[pl.ds(b * (nz * rd) + y, nz, stride=rd), :]
            state_a[b, y] = row
            rows.append([row[block(g)] for g in range(groups)])
            if y == 0:
                row_out[0, UP, b] = row.astype(BF16)
            if y == rd - 1:
                row_out[0, DOWN, b] = row.astype(BF16)
        col_out[0, b] = pack(rows)
        return 0

    lax.fori_loop(0, bins, first_pack, 0)

    diag = lax.broadcasted_iota(jnp.int32, (nz, nz), 0) == lax.broadcasted_iota(
        jnp.int32, (nz, nz), 1
    )
    low = jnp.sum(
        jnp.where(diag, lev_lo[...].astype(F32), 0.0), axis=1, keepdims=True
    ).astype(jnp.int32)
    share = jnp.sum(jnp.where(diag, frac[...], 0.0), axis=1, keepdims=True)
    level_id = lax.broadcasted_iota(jnp.int32, (nz, ln), 1)
    interp = jnp.where(level_id == low, 1.0 - share, 0.0) + jnp.where(
        level_id == low + 1, share, 0.0
    )
    interp_hi = interp.astype(BF16)
    rest = interp - interp_hi.astype(F32)
    interp_mid = rest.astype(BF16)
    interp_lo = (rest - interp_mid.astype(F32)).astype(BF16)
    parts = jnp.concatenate([interp_hi, interp_mid, interp_lo], axis=0)
    for f in range(2):
        mixed = jnp.dot(parts, nwp[f], preferred_element_type=F32)
        levels[f * nz : (f + 1) * nz, :] = (
            mixed[:nz] + mixed[nz : 2 * nz] + mixed[2 * nz :]
        ).astype(BF16)

    def band_copy(source, dest, d):
        return pltpu.make_async_remote_copy(
            src_ref=sent.at[pl.ds(pl.multiple_of(dest * cap, cap), cap)],
            dst_ref=got.at[pl.ds(pl.multiple_of(source * cap, cap), cap)],
            send_sem=band_send.at[d],
            recv_sem=band_recv.at[d],
            device_id={"rows": dest},
            device_id_type=MESH,
        )

    per = 4
    width = per * cap

    def choose(p, _):
        wanted = jnp.concatenate([pick[0, 0, pl.ds(p * per + i, 1), :] for i in range(per)], axis=1)
        step = 128

        def fill(t, _):
            ids = lax.broadcasted_iota(jnp.int32, (step, width), 0) + t * step
            onehot[pl.ds(t * step, step), :] = jnp.where(ids == wanted, 1.0, 0.0).astype(BF16)
            return 0

        lax.fori_loop(0, columns // step, fill, 0)
        chosen = jnp.dot(levels[...], onehot[...], preferred_element_type=F32)
        chosen = jnp.concatenate([chosen, jnp.zeros((128 - 2 * nz, width), F32)], axis=0)
        sent[pl.ds(p * width, width), :] = chosen.T.astype(BF16)
        return 0

    lax.fori_loop(0, n_rows // per, choose, 0)
    pl.semaphore_wait(
        barrier, n_rows - 1 + has[LEFT].astype(jnp.int32) + has[RIGHT].astype(jnp.int32)
    )
    for d in range(1, n_rows):
        band_copy(r, lax.rem(r + d, n_rows), d).start()

    def first_send(b, _):
        send_halo(0, b)
        return 0

    lax.fori_loop(0, bins, first_send, 0)

    weights = corner_wt[...]
    norm_wt[...] = weights / (weights[0] + weights[1] + weights[2] + weights[3])
    chunk = 128

    def fill_table(i, _):
        p = i // (slots // chunk)
        t = i % (slots // chunk)
        ids = lax.broadcasted_iota(jnp.int32, (chunk, cd), 0) + t * chunk
        for half in range(2):
            total = jnp.zeros((chunk, cd), F32)
            for q in range(4):
                slot = corner_slot[q, pl.ds(2 * p + half, 1), :]
                wt = norm_wt[q, pl.ds(2 * p + half, 1), :]
                total = total + jnp.where(ids == slot, wt, 0.0)
            hi = total.astype(BF16)
            where = (p, pl.ds(t * chunk, chunk), pl.ds(half * cd, cd))
            table_hi[where] = hi
            table_lo[where] = (total - hi.astype(F32)).astype(BF16)
        return 0

    lax.fori_loop(0, (rd // 2) * (slots // chunk), fill_table, 0)

    own = pl.ds(pl.multiple_of(r * cap, cap), cap)
    got[own, :] = sent[own, :]
    for d in range(1, n_rows):
        band_copy(lax.rem(r + n_rows - d, n_rows), r, d).wait_recv()
    for t in range(slots // 128):
        turned[:, t * 128 : (t + 1) * 128] = (
            got[t * 128 : (t + 1) * 128, :].astype(F32).T.astype(BF16)
        )
    for p in range(rd // 2):
        blown = jnp.dot(turned[...], table_hi[p], preferred_element_type=F32) + jnp.dot(
            turned[...], table_lo[p], preferred_element_type=F32
        )
        winds[2 * p] = blown[: 2 * nz, :cd]
        winds[2 * p + 1] = blown[: 2 * nz, cd:]

    wind_row_out[UP] = winds[0, nz:, :].astype(BF16)
    wind_row_out[DOWN] = winds[rd - 1, nz:, :].astype(BF16)
    wind_col_out[...] = pack([[winds[y, block(g), :] for g in range(groups)] for y in range(rd)])
    for side in range(4):

        @pl.when(has[side])
        def _():
            wind_copy(side).start()

    for side in range(4):

        @pl.when(has[side])
        def _():
            wind_arrival(side).wait_recv()

    def across(plane, rim, y, g):
        rim = pltpu.roll(rim, cd - 2 * (y * groups + g) - 1, 1)
        ahead = jnp.where(last_lane, rim, pltpu.roll(plane, cd - 1, 1))
        behind = jnp.where(first_lane, rim, pltpu.roll(plane, 1, 1))
        return ahead, behind

    wind_rim = unpack(wind_col_in[0], wind_col_in[1])
    wind_rows = (
        [wind_row_in[UP].astype(F32)]
        + [winds[y, nz:, :] for y in range(rd)]
        + [wind_row_in[DOWN].astype(F32)]
    )
    for y in range(rd):
        for g in range(groups):
            k = block(g)
            u = winds[y, k, :]
            u_ahead, u_behind = across(u, wind_rim, y, g)
            v_above, v, v_below = (wind_rows[y + i][k] for i in range(3))
            right, left = 0.5 * (u + u_ahead), 0.5 * (u + u_behind)
            down, up = 0.5 * (v + v_below), 0.5 * (v + v_above)
            coef[0, y, k, :] = (
                (1.0 - 4.0 * KAPPA)
                - jnp.maximum(right, 0.0)
                + jnp.minimum(left, 0.0)
                - jnp.maximum(down, 0.0)
                + jnp.minimum(up, 0.0)
            )
            coef[1, y, k, :] = KAPPA - jnp.minimum(right, 0.0)
            coef[2, y, k, :] = KAPPA + jnp.maximum(left, 0.0)
            coef[3, y, k, :] = KAPPA - jnp.minimum(down, 0.0)
            coef[4, y, k, :] = KAPPA + jnp.maximum(up, 0.0)

    diag = lax.broadcasted_iota(jnp.int32, (nz, nz), 0) == lax.broadcasted_iota(
        jnp.int32, (nz, nz), 1
    )
    for b in range(bins):
        column = jnp.sum(jnp.where(diag, profile[b : b + 1, :], 0.0), axis=1, keepdims=True)
        spread[b] = jnp.broadcast_to(column, (nz, cd))
    flags[...] = source_mask[...].astype(F32)
    flat_out = out.reshape(bins * nz * rd, cd)
    for stage in range(STEPS):
        src = (state_a, state_b)[stage % 2]
        dst = (state_b, state_a)[stage % 2]
        last = stage == STEPS - 1

        def one_bin(b, _):
            for side in range(4):

                @pl.when(has[side])
                def _():
                    halo_arrival(stage, side, b).wait_recv()

            rim = unpack(col_in[stage, 0, b], col_in[stage, 1, b])
            sink = settle[b]
            rows = (
                [row_in[stage, UP, b].astype(F32)]
                + [src[b, y] for y in range(rd)]
                + [row_in[stage, DOWN, b].astype(F32)]
            )
            fresh = []
            for y in range(rd):
                flag = flags[y : y + 1, :]
                news = []
                turned_over = jnp.zeros((rd, cd), F32)
                for g in range(groups):
                    k = block(g)
                    above, a, below = (rows[y + i][k] for i in range(3))
                    ahead, behind = across(a, rim, y, g)
                    falling = sink * a
                    rolled = pltpu.roll(falling, 1, 0)
                    arriving = jnp.where(first_sub, turned_over, rolled)
                    turned_over = rolled
                    new = (
                        (coef[0, y, k, :] * a + coef[1, y, k, :] * ahead)
                        + (coef[2, y, k, :] * behind + coef[3, y, k, :] * below)
                        + (coef[4, y, k, :] * above + flag * spread[b, k, :])
                        + (arriving - falling)
                    )
                    if last:
                        flat_out[pl.ds(b * (nz * rd) + g * (rd * rd) + y, rd, stride=rd), :] = new
                    else:
                        dst[b, y, k, :] = new
                    news.append(new)
                fallen = falling[rd - 1 :, :]
                here_row = (b, slice(y, y + 1), slice(None))
                deposit[here_row] = fallen if stage == 0 else deposit[here_row] + fallen
                fresh.append(news)
                if not last and y == 0:
                    row_out[stage + 1, UP, b] = jnp.concatenate(news, axis=0).astype(BF16)
            if not last:
                row_out[stage + 1, DOWN, b] = jnp.concatenate(fresh[-1], axis=0).astype(BF16)
                col_out[stage + 1, b] = pack(fresh)
                send_halo(stage + 1, b)
            return 0

        lax.fori_loop(0, bins, one_bin, 0)

    for d in range(1, n_rows):
        band_copy(r, lax.rem(r + d, n_rows), d).wait_send()
    for side in range(4):

        @pl.when(has[side])
        def _():
            wind_copy(side).wait_send()

            def drain(b, _):
                for stage in range(STEPS):
                    halo_copy(stage, side, b).wait_send()
                return 0

            lax.fori_loop(0, bins, drain, 0)


def per_device(conc, nwp, lev_lo, frac, pick, corner_slot, corner_wt, settle, source_mask, profile):
    n_rows, n_cols = lax.axis_size("rows"), lax.axis_size("cols")
    bins, nz, rd, cd = conc.shape
    cap = pick.shape[3]
    slots = n_rows * cap
    columns = nwp.shape[2]
    vmem = pl.BlockSpec(memory_space=pltpu.VMEM)
    smem = pl.BlockSpec(memory_space=pltpu.SMEM)
    return pl.pallas_call(
        functools.partial(kernel, n_rows, n_cols),
        out_shape=(
            jax.ShapeDtypeStruct(conc.shape, F32),
            jax.ShapeDtypeStruct((bins, rd, cd), F32),
        ),
        in_specs=[vmem] * 7 + [smem, vmem, vmem],
        out_specs=(vmem, vmem),
        scratch_shapes=[
            pltpu.VMEM((2 * nz, columns), BF16),
            pltpu.VMEM((columns, 4 * cap), BF16),
            pltpu.VMEM((slots, 128), BF16),
            pltpu.VMEM((slots, 128), BF16),
            pltpu.VMEM((128, slots), BF16),
            pltpu.VMEM(corner_wt.shape, F32),
            pltpu.VMEM((rd // 2, slots, 2 * cd), BF16),
            pltpu.VMEM((rd // 2, slots, 2 * cd), BF16),
            pltpu.VMEM((rd, 2 * nz, cd), F32),
            pltpu.VMEM((2, nz, cd), BF16),
            pltpu.VMEM((2, nz, cd), BF16),
            pltpu.VMEM((rd, cd), F32),
            pltpu.VMEM((2, rd, cd), F32),
            pltpu.VMEM((STEPS, 2, bins, nz, cd), BF16),
            pltpu.VMEM((STEPS, 2, bins, nz, cd), BF16),
            pltpu.VMEM((STEPS, bins, rd, cd), F32),
            pltpu.VMEM((STEPS, 2, bins, rd, cd), F32),
            pltpu.VMEM((5, rd, nz, cd), F32),
            pltpu.VMEM((bins, rd, nz, cd), F32),
            pltpu.VMEM((bins, rd, nz, cd), F32),
            pltpu.VMEM((bins, nz, cd), F32),
            pltpu.VMEM((rd, cd), F32),
            pltpu.SemaphoreType.DMA((n_rows,)),
            pltpu.SemaphoreType.DMA((n_rows,)),
            pltpu.SemaphoreType.DMA((4,)),
            pltpu.SemaphoreType.DMA((4,)),
            pltpu.SemaphoreType.DMA((STEPS, 4, bins)),
            pltpu.SemaphoreType.DMA((STEPS, 4, bins)),
        ],
        compiler_params=pltpu.CompilerParams(
            collective_id=0, has_side_effects=True, vmem_limit_bytes=48 * 1024 * 1024
        ),
        cost_estimate=pl.CostEstimate(
            flops=10**9, bytes_accessed=6 * 10**6, transcendentals=0
        ),
        name="ash",
    )(
        conc,
        nwp,
        lev_lo.reshape(1, -1),
        frac.reshape(1, -1),
        pick,
        corner_slot,
        corner_wt,
        settle,
        source_mask,
        profile,
    )


def solution(mesh):
    placed = (
        P(None, None, "rows", "cols"),
        P(None, None, "rows"),
        P(),
        P(),
        P("rows", "cols", None, None),
        P(None, "rows", "cols"),
        P(None, "rows", "cols"),
        P(),
        P("rows", "cols"),
        P(),
    )
    return jax.shard_map(
        per_device,
        mesh=mesh,
        in_specs=placed,
        out_specs=(P(None, None, "rows", "cols"), P(None, "rows", "cols")),
        check_vma=False,
    )
```

```python
import functools

import jax
import jax.numpy as jnp
from jax import lax
from jax.experimental import pallas as pl
from jax.experimental.pallas import tpu as pltpu
from jax.sharding import PartitionSpec as P

STEPS = 3
KAPPA = 0.05
MESH = pl.DeviceIdType.MESH
UP, DOWN, LEFT, RIGHT = range(4)
BF16 = jnp.bfloat16
F32 = jnp.float32


def kernel(
    n_rows,
    n_cols,
    conc,
    nwp,
    lev_lo,
    frac,
    pick,
    corner_slot,
    corner_wt,
    settle,
    source_mask,
    profile,
    out,
    deposit,
    levels,
    onehot,
    sent,
    got,
    turned,
    norm_wt,
    table_hi,
    table_lo,
    winds,
    wind_row_out,
    wind_row_in,
    wind_col_out,
    wind_col_in,
    wind_diag_in,
    flag_out,
    flag_in,
    row_out,
    row_in,
    col_out,
    col_in,
    coef,
    state_a,
    state_b,
    spread,
    flags,
    band_send,
    band_recv,
    wind_send,
    wind_recv,
    diag_send,
    diag_recv,
    flag_send,
    flag_recv,
    row_send,
    row_recv,
    col_send,
    col_recv,
):
    bins, nz, rd, cd = conc.shape
    ln, columns = nwp.shape[1:]
    cap = pick.shape[3]
    slots = n_rows * cap
    r = lax.axis_index("rows")
    c = lax.axis_index("cols")
    has = (r > 0, r < n_rows - 1, c > 0, c < n_cols - 1)
    target = ({"rows": r - 1}, {"rows": r + 1}, {"cols": c - 1}, {"cols": c + 1})
    lane = lax.broadcasted_iota(jnp.int32, (rd, cd), 1)
    sub = lax.broadcasted_iota(jnp.int32, (rd, cd), 0)
    odd = (lane % 2) == 1
    first_lane, last_lane = lane == 0, lane == cd - 1
    first_sub = sub == 0
    corners = [(v, h) for v in (UP, DOWN) for h in (LEFT, RIGHT)]
    has_corner = [has[v] & has[h] for v, h in corners]
    to_corner = [{**target[v], **target[h]} for v, h in corners]

    barrier = pltpu.get_barrier_semaphore()
    for d in range(1, n_rows):
        pl.semaphore_signal(
            barrier, inc=1, device_id={"rows": lax.rem(r + d, n_rows)}, device_id_type=MESH
        )
    for side in (LEFT, RIGHT):

        @pl.when(has[side])
        def _():
            pl.semaphore_signal(barrier, inc=1, device_id=target[side], device_id_type=MESH)

    for i in range(4):

        @pl.when(has_corner[i])
        def _():
            pl.semaphore_signal(barrier, inc=1, device_id=to_corner[i], device_id_type=MESH)

    for side in (UP, DOWN):

        @pl.when(jnp.logical_not(has[side]))
        def _():
            row_in[side] = jnp.zeros(row_in.shape[1:], BF16)
            wind_row_in[side] = jnp.zeros(wind_row_in.shape[1:], BF16)
            flag_in[side] = jnp.zeros(flag_in.shape[1:], BF16)

    for side in (LEFT, RIGHT):

        @pl.when(jnp.logical_not(has[side]))
        def _():
            col_in[side - 2] = jnp.zeros(col_in.shape[1:], F32)
            wind_col_in[side - 2] = jnp.zeros(wind_col_in.shape[1:], F32)

    for i in range(4):

        @pl.when(jnp.logical_not(has_corner[i]))
        def _():
            wind_diag_in[i] = jnp.zeros((rd, cd), F32)

    groups = nz // rd
    here = [(lane // 2) == g for g in range(groups)]

    def block(g):
        return slice(g * rd, (g + 1) * rd)

    def pack(rows):
        packed = jnp.zeros((rd, cd), F32)
        for i, row in rows:
            acc = jnp.zeros((rd, cd), F32)
            for g in range(groups):
                acc = jnp.where(here[g], pltpu.roll(row[g], 2 * g + 1, 1), acc)
            packed = packed + (pltpu.roll(acc, 2 * groups * i, 1) if i else acc)
        return packed

    def split(row):
        return [row[block(g)] for g in range(groups)]

    def unpack(left, right):
        return jnp.where(odd, pltpu.roll(left, 1, 1), pltpu.roll(right, cd - 1, 1))

    def push(side, src, dst, send_sem, recv_sem):
        return pltpu.make_async_remote_copy(
            src_ref=src,
            dst_ref=dst,
            send_sem=send_sem,
            recv_sem=recv_sem,
            device_id=target[side],
            device_id_type=MESH,
        )

    def row_copy(side, b, arrival=False):
        end = side if arrival else side ^ 1
        return push(
            side, row_out.at[side, b], row_in.at[end, b], row_send.at[side, b], row_recv.at[end, b]
        )

    def col_copy(kind, side, b, arrival=False):
        end = (side if arrival else side ^ 1) - 2
        return push(
            side,
            col_out.at[kind, b],
            col_in.at[end, kind, b],
            col_send.at[kind, side - 2, b],
            col_recv.at[kind, end, b],
        )

    def flag_copy(side, arrival=False):
        end = side if arrival else side ^ 1
        return push(side, flag_out, flag_in.at[end], flag_send.at[side], flag_recv.at[end])

    def wind_copy(side, arrival=False):
        end = side if arrival else side ^ 1
        if side < 2:
            src, dst = wind_row_out.at[side], wind_row_in.at[end]
        else:
            src, dst = wind_col_out, wind_col_in.at[end - 2]
        return push(side, src, dst, wind_send.at[side], wind_recv.at[end])

    def diag_copy(i, arrival=False):
        end = i if arrival else 3 - i
        return pltpu.make_async_remote_copy(
            src_ref=wind_col_out,
            dst_ref=wind_diag_in.at[end],
            send_sem=diag_send.at[i],
            recv_sem=diag_recv.at[end],
            device_id=to_corner[i],
            device_id_type=MESH,
        )

    def each(sides, act):
        for side in sides:

            @pl.when(has[side])
            def _():
                act(side)

    def send_rows(first, end):
        def one(b, _):
            each((UP, DOWN), lambda side: row_copy(side, b).start())
            return 0

        lax.fori_loop(first, end, one, 0)

    def send_cols(kind, b):
        each((LEFT, RIGHT), lambda side: col_copy(kind, side, b).start())

    flat_conc = conc.reshape(bins * nz * rd, cd)
    margin = STEPS
    reach = margin - 1

    def first_pack(b, _):
        rows = []
        for y in range(rd):
            row = flat_conc[pl.ds(b * (nz * rd) + y, nz, stride=rd), :]
            state_a[b, y + reach] = row
            rows.append((y, split(row)))
            if y < margin:
                row_out[UP, b, y * nz : (y + 1) * nz, :] = row.astype(BF16)
            if rd - 1 - y < margin:
                i = rd - 1 - y
                row_out[DOWN, b, i * nz : (i + 1) * nz, :] = row.astype(BF16)
        col_out[0, b] = pack(rows)
        return 0

    lax.fori_loop(0, bins, first_pack, 0)
    mask = source_mask[...].astype(F32)
    flags[reach : reach + rd, :] = mask
    flag_out[...] = jnp.concatenate([mask, jnp.zeros_like(mask)], axis=0).astype(BF16)

    def count(flag):
        return flag.astype(jnp.int32)

    pl.semaphore_wait(
        barrier,
        n_rows - 1 + count(has[LEFT]) + count(has[RIGHT]) + sum(count(h) for h in has_corner),
    )
    early, middle = (3 * bins) // 8, (6 * bins) // 8
    each((UP, DOWN), lambda side: flag_copy(side).start())
    send_rows(0, early)

    def first_cols(b, _):
        send_cols(0, b)
        return 0

    lax.fori_loop(0, bins, first_cols, 0)

    diag = lax.broadcasted_iota(jnp.int32, (nz, nz), 0) == lax.broadcasted_iota(
        jnp.int32, (nz, nz), 1
    )
    low = jnp.sum(
        jnp.where(diag, lev_lo[...].astype(F32), 0.0), axis=1, keepdims=True
    ).astype(jnp.int32)
    share = jnp.sum(jnp.where(diag, frac[...], 0.0), axis=1, keepdims=True)
    level_id = lax.broadcasted_iota(jnp.int32, (nz, ln), 1)
    interp = jnp.where(level_id == low, 1.0 - share, 0.0) + jnp.where(
        level_id == low + 1, share, 0.0
    )
    interp_hi = interp.astype(BF16)
    rest = interp - interp_hi.astype(F32)
    interp_mid = rest.astype(BF16)
    interp_lo = (rest - interp_mid.astype(F32)).astype(BF16)
    parts = jnp.concatenate([interp_hi, interp_mid, interp_lo], axis=0)
    for f in range(2):
        mixed = jnp.dot(parts, nwp[f], preferred_element_type=F32)
        levels[f * nz : (f + 1) * nz, :] = (
            mixed[:nz] + mixed[nz : 2 * nz] + mixed[2 * nz :]
        ).astype(BF16)

    def band_copy(source, dest, d):
        return pltpu.make_async_remote_copy(
            src_ref=sent.at[pl.ds(pl.multiple_of(dest * cap, cap), cap)],
            dst_ref=got.at[pl.ds(pl.multiple_of(source * cap, cap), cap)],
            send_sem=band_send.at[d],
            recv_sem=band_recv.at[d],
            device_id={"rows": dest},
            device_id_type=MESH,
        )

    per = 4
    width = per * cap

    def choose(p, _):
        wanted = jnp.concatenate([pick[0, 0, pl.ds(p * per + i, 1), :] for i in range(per)], axis=1)
        step = 128

        def fill(t, _):
            ids = lax.broadcasted_iota(jnp.int32, (step, width), 0) + t * step
            onehot[pl.ds(t * step, step), :] = jnp.where(ids == wanted, 1.0, 0.0).astype(BF16)
            return 0

        lax.fori_loop(0, columns // step, fill, 0)
        chosen = jnp.dot(levels[...], onehot[...], preferred_element_type=F32)
        chosen = jnp.concatenate([chosen, jnp.zeros((128 - 2 * nz, width), F32)], axis=0)
        sent[pl.ds(p * width, width), :] = chosen.T.astype(BF16)
        return 0

    lax.fori_loop(0, n_rows // per, choose, 0)
    for d in range(1, n_rows):
        band_copy(r, lax.rem(r + d, n_rows), d).start()

    send_rows(early, middle)

    weights = corner_wt[...]
    norm_wt[...] = weights / (weights[0] + weights[1] + weights[2] + weights[3])
    chunk = 128

    def fill_table(i, _):
        p = i // (slots // chunk)
        t = i % (slots // chunk)
        ids = lax.broadcasted_iota(jnp.int32, (chunk, cd), 0) + t * chunk
        for half in range(2):
            total = jnp.zeros((chunk, cd), F32)
            for q in range(4):
                slot = corner_slot[q, pl.ds(2 * p + half, 1), :]
                wt = norm_wt[q, pl.ds(2 * p + half, 1), :]
                total = total + jnp.where(ids == slot, wt, 0.0)
            hi = total.astype(BF16)
            where = (p, pl.ds(t * chunk, chunk), pl.ds(half * cd, cd))
            table_hi[where] = hi
            table_lo[where] = (total - hi.astype(F32)).astype(BF16)
        return 0

    lax.fori_loop(0, (rd // 2) * (slots // chunk), fill_table, 0)

    diag = lax.broadcasted_iota(jnp.int32, (nz, nz), 0) == lax.broadcasted_iota(
        jnp.int32, (nz, nz), 1
    )
    for b in range(bins):
        column = jnp.sum(jnp.where(diag, profile[b : b + 1, :], 0.0), axis=1, keepdims=True)
        spread[b] = jnp.broadcast_to(column, (nz, cd))

    own = pl.ds(pl.multiple_of(r * cap, cap), cap)
    got[own, :] = sent[own, :]
    for d in range(1, n_rows):
        band_copy(lax.rem(r + n_rows - d, n_rows), r, d).wait_recv()
    for t in range(slots // 128):
        turned[:, t * 128 : (t + 1) * 128] = (
            got[t * 128 : (t + 1) * 128, :].astype(F32).T.astype(BF16)
        )
    for p in range(rd // 2):
        blown = jnp.dot(turned[...], table_hi[p], preferred_element_type=F32) + jnp.dot(
            turned[...], table_lo[p], preferred_element_type=F32
        )
        winds[2 * p] = blown[: 2 * nz, :cd]
        winds[2 * p + 1] = blown[: 2 * nz, cd:]

    for side, order in ((UP, range(reach + 1)), (DOWN, range(rd - 1, rd - 2 - reach, -1))):
        for i, y in enumerate(order):
            kept = winds[y] if i < reach else winds[y, nz:, :]
            wind_row_out[side, 2 * i * nz : 2 * i * nz + kept.shape[0], :] = kept.astype(BF16)
    wind_col_out[...] = pack(
        [(y, [winds[y, block(g), :] for g in range(groups)]) for y in range(rd)]
    )
    each(range(4), lambda side: wind_copy(side).start())
    for i in range(4):

        @pl.when(has_corner[i])
        def _():
            diag_copy(i).start()

    send_rows(middle, bins)

    def outer_cols(b):
        each((UP, DOWN), lambda side: row_copy(side, b, arrival=True).wait_recv())
        rows = []
        for i in range(reach):
            k = slice(i * nz, (i + 1) * nz)
            rows.append((reach - 1 - i, split(row_in[UP, b, k, :].astype(F32))))
            rows.append((reach + i, split(row_in[DOWN, b, k, :].astype(F32))))
        col_out[1, b] = pack(rows)
        send_cols(1, b)

    ahead_of = min(3, bins)

    def first_outer(b, _):
        outer_cols(b)
        return 0

    lax.fori_loop(0, ahead_of, first_outer, 0)
    each((UP, DOWN), lambda side: flag_copy(side, arrival=True).wait_recv())
    flags[:reach, :] = flag_in[UP].astype(F32)[rd - reach : rd]
    flags[reach + rd : reach + rd + reach, :] = flag_in[DOWN].astype(F32)[:reach]
    each(range(4), lambda side: wind_copy(side, arrival=True).wait_recv())
    for i in range(4):

        @pl.when(has_corner[i])
        def _():
            diag_copy(i, arrival=True).wait_recv()

    def across(plane, rim, i, g):
        rim = pltpu.roll(rim, cd - 2 * (i * groups + g) - 1, 1)
        ahead = jnp.where(last_lane, rim, pltpu.roll(plane, cd - 1, 1))
        behind = jnp.where(first_lane, rim, pltpu.roll(plane, 1, 1))
        return ahead, behind

    def outer_wind(side, i, f):
        return wind_row_in[side, (2 * i + f) * nz : (2 * i + f + 1) * nz, :].astype(F32)

    last_row = [
        wind_row_in[side, 2 * reach * nz : (2 * reach + 1) * nz, :].astype(F32)
        for side in (UP, DOWN)
    ]
    easts = (
        [outer_wind(UP, i, 0) for i in reversed(range(reach))]
        + [winds[y, :nz, :] for y in range(rd)]
        + [outer_wind(DOWN, i, 0) for i in range(reach)]
    )
    norths = (
        [last_row[0]]
        + [outer_wind(UP, i, 1) for i in reversed(range(reach))]
        + [winds[y, nz:, :] for y in range(rd)]
        + [outer_wind(DOWN, i, 1) for i in range(reach)]
        + [last_row[1]]
    )
    wind_rim = unpack(wind_col_in[0], wind_col_in[1])
    upper_rim = unpack(wind_diag_in[0], wind_diag_in[1])
    lower_rim = unpack(wind_diag_in[2], wind_diag_in[3])
    for y in range(-reach, rd + reach):
        at = y + reach
        rim, i = (
            (upper_rim, y + rd) if y < 0 else (wind_rim, y) if y < rd else (lower_rim, y - rd)
        )
        for g in range(groups):
            k = block(g)
            u = easts[at][k]
            u_ahead, u_behind = across(u, rim, i, g)
            v_above, v, v_below = (norths[at + i][k] for i in range(3))
            right, left = 0.5 * (u + u_ahead), 0.5 * (u + u_behind)
            down, up = 0.5 * (v + v_below), 0.5 * (v + v_above)
            coef[0, at, k, :] = (
                (1.0 - 4.0 * KAPPA)
                - jnp.maximum(right, 0.0)
                + jnp.minimum(left, 0.0)
                - jnp.maximum(down, 0.0)
                + jnp.minimum(up, 0.0)
            )
            coef[1, at, k, :] = KAPPA - jnp.minimum(right, 0.0)
            coef[2, at, k, :] = KAPPA + jnp.maximum(left, 0.0)
            coef[3, at, k, :] = KAPPA - jnp.minimum(down, 0.0)
            coef[4, at, k, :] = KAPPA + jnp.maximum(up, 0.0)

    keep = [has[UP].astype(F32), has[DOWN].astype(F32)]
    flat_out = out.reshape(bins * nz * rd, cd)
    for stage in range(STEPS):
        src = (state_a, state_b)[stage % 2]
        dst = (state_b, state_a)[stage % 2]
        last = stage == STEPS - 1

        def one_bin(b, _):
            if stage == 0:

                @pl.when(b + ahead_of < bins)
                def _():
                    outer_cols(b + ahead_of)

            kinds = (2 * stage,) if last else (2 * stage, 2 * stage + 1)
            for kind in kinds:
                each((LEFT, RIGHT), lambda side: col_copy(kind, side, b, arrival=True).wait_recv())
            rims = [unpack(col_in[0, kind, b], col_in[1, kind, b]) for kind in kinds]
            sink = settle[b]
            grow = reach - stage

            def source(y):
                if stage == 0 and y < 0:
                    return row_in[UP, b, (-1 - y) * nz : -y * nz, :].astype(F32)
                if stage == 0 and y >= rd:
                    return row_in[DOWN, b, (y - rd) * nz : (y - rd + 1) * nz, :].astype(F32)
                return src[b, y + reach]

            rows = [source(y) for y in range(-grow - 1, rd + grow + 1)]
            fresh = []
            outer = []
            for y in range(-grow, rd + grow):
                main = 0 <= y < rd
                at = y + reach
                flag = flags[at : at + 1, :]
                news = []
                turned_over = jnp.zeros((rd, cd), F32)
                for g in range(groups):
                    k = block(g)
                    above, a, below = (rows[y + grow + i][k] for i in range(3))
                    if main:
                        ahead, behind = across(a, rims[0], y, g)
                    else:
                        ahead, behind = across(a, rims[1], at if y < 0 else at - rd, g)
                    falling = sink * a
                    rolled = pltpu.roll(falling, 1, 0)
                    arriving = jnp.where(first_sub, turned_over, rolled)
                    turned_over = rolled
                    new = (
                        (coef[0, at, k, :] * a + coef[1, at, k, :] * ahead)
                        + (coef[2, at, k, :] * behind + coef[3, at, k, :] * below)
                        + (coef[4, at, k, :] * above + flag * spread[b, k, :])
                        + (arriving - falling)
                    )
                    if not main:
                        new = new * keep[0 if y < 0 else 1]
                    if last:
                        flat_out[pl.ds(b * (nz * rd) + g * (rd * rd) + y, rd, stride=rd), :] = new
                    else:
                        dst[b, at, k, :] = new
                    news.append(new)
                if main:
                    fallen = falling[rd - 1 :, :]
                    here_row = (b, slice(y, y + 1), slice(None))
                    deposit[here_row] = fallen if stage == 0 else deposit[here_row] + fallen
                    fresh.append((y, news))
                elif -grow < y < rd + grow - 1:
                    outer.append((at if y < 0 else at - rd, news))
            if not last:
                col_out[2 * stage + 2, b] = pack(fresh)
                send_cols(2 * stage + 2, b)
            if outer:
                col_out[2 * stage + 3, b] = pack(outer)
                send_cols(2 * stage + 3, b)
            return 0

        lax.fori_loop(0, bins, one_bin, 0)

    for d in range(1, n_rows):
        band_copy(r, lax.rem(r + d, n_rows), d).wait_send()
    each(range(4), lambda side: wind_copy(side).wait_send())
    for i in range(4):

        @pl.when(has_corner[i])
        def _():
            diag_copy(i).wait_send()

    each((UP, DOWN), lambda side: flag_copy(side).wait_send())

    def drain(b, _):
        each((UP, DOWN), lambda side: row_copy(side, b).wait_send())
        for kind in range(2 * STEPS - 1):
            each((LEFT, RIGHT), lambda side: col_copy(kind, side, b).wait_send())
        return 0

    lax.fori_loop(0, bins, drain, 0)


def per_device(conc, nwp, lev_lo, frac, pick, corner_slot, corner_wt, settle, source_mask, profile):
    n_rows, n_cols = lax.axis_size("rows"), lax.axis_size("cols")
    bins, nz, rd, cd = conc.shape
    cap = pick.shape[3]
    slots = n_rows * cap
    columns = nwp.shape[2]
    tall = rd + 2 * (STEPS - 1)
    vmem = pl.BlockSpec(memory_space=pltpu.VMEM)
    smem = pl.BlockSpec(memory_space=pltpu.SMEM)
    return pl.pallas_call(
        functools.partial(kernel, n_rows, n_cols),
        out_shape=(
            jax.ShapeDtypeStruct(conc.shape, F32),
            jax.ShapeDtypeStruct((bins, rd, cd), F32),
        ),
        in_specs=[vmem] * 7 + [smem, vmem, vmem],
        out_specs=(vmem, vmem),
        scratch_shapes=[
            pltpu.VMEM((2 * nz, columns), BF16),
            pltpu.VMEM((columns, 4 * cap), BF16),
            pltpu.VMEM((slots, 128), BF16),
            pltpu.VMEM((slots, 128), BF16),
            pltpu.VMEM((128, slots), BF16),
            pltpu.VMEM(corner_wt.shape, F32),
            pltpu.VMEM((rd // 2, slots, 2 * cd), BF16),
            pltpu.VMEM((rd // 2, slots, 2 * cd), BF16),
            pltpu.VMEM((rd, 2 * nz, cd), F32),
            pltpu.VMEM((2, (2 * STEPS - 1) * nz, cd), BF16),
            pltpu.VMEM((2, (2 * STEPS - 1) * nz, cd), BF16),
            pltpu.VMEM((rd, cd), F32),
            pltpu.VMEM((2, rd, cd), F32),
            pltpu.VMEM((4, rd, cd), F32),
            pltpu.VMEM((2 * rd, cd), BF16),
            pltpu.VMEM((2, 2 * rd, cd), BF16),
            pltpu.VMEM((2, bins, STEPS * nz, cd), BF16),
            pltpu.VMEM((2, bins, STEPS * nz, cd), BF16),
            pltpu.VMEM((2 * STEPS - 1, bins, rd, cd), F32),
            pltpu.VMEM((2, 2 * STEPS - 1, bins, rd, cd), F32),
            pltpu.VMEM((5, tall, nz, cd), F32),
            pltpu.VMEM((bins, tall, nz, cd), F32),
            pltpu.VMEM((bins, tall, nz, cd), F32),
            pltpu.VMEM((bins, nz, cd), F32),
            pltpu.VMEM((2 * rd, cd), F32),
            pltpu.SemaphoreType.DMA((n_rows,)),
            pltpu.SemaphoreType.DMA((n_rows,)),
            pltpu.SemaphoreType.DMA((4,)),
            pltpu.SemaphoreType.DMA((4,)),
            pltpu.SemaphoreType.DMA((4,)),
            pltpu.SemaphoreType.DMA((4,)),
            pltpu.SemaphoreType.DMA((2,)),
            pltpu.SemaphoreType.DMA((2,)),
            pltpu.SemaphoreType.DMA((2, bins)),
            pltpu.SemaphoreType.DMA((2, bins)),
            pltpu.SemaphoreType.DMA((2 * STEPS - 1, 2, bins)),
            pltpu.SemaphoreType.DMA((2 * STEPS - 1, 2, bins)),
        ],
        compiler_params=pltpu.CompilerParams(
            collective_id=0, has_side_effects=True, vmem_limit_bytes=48 * 1024 * 1024
        ),
        cost_estimate=pl.CostEstimate(
            flops=10**9, bytes_accessed=6 * 10**6, transcendentals=0
        ),
        name="ash",
    )(
        conc,
        nwp,
        lev_lo.reshape(1, -1),
        frac.reshape(1, -1),
        pick,
        corner_slot,
        corner_wt,
        settle,
        source_mask,
        profile,
    )


def solution(mesh):
    placed = (
        P(None, None, "rows", "cols"),
        P(None, None, "rows"),
        P(),
        P(),
        P("rows", "cols", None, None),
        P(None, "rows", "cols"),
        P(None, "rows", "cols"),
        P(),
        P("rows", "cols"),
        P(),
    )
    return jax.shard_map(
        per_device,
        mesh=mesh,
        in_specs=placed,
        out_specs=(P(None, None, "rows", "cols"), P(None, "rows", "cols")),
        check_vma=False,
    )
```

```python
import functools

import jax
import jax.numpy as jnp
from jax import lax
from jax.experimental import pallas as pl
from jax.experimental.pallas import tpu as pltpu
from jax.sharding import PartitionSpec as P

STEPS = 3
KAPPA = 0.05
MESH = pl.DeviceIdType.MESH
UP, DOWN, LEFT, RIGHT = range(4)
BF16 = jnp.bfloat16
F32 = jnp.float32


def kernel(
    n_rows,
    n_cols,
    conc,
    nwp,
    lev_lo,
    frac,
    pick,
    corner_slot,
    corner_wt,
    settle,
    source_mask,
    profile,
    out,
    deposit,
    levels,
    onehot,
    sent,
    got,
    turned,
    norm_wt,
    table_hi,
    table_lo,
    winds,
    wind_row_out,
    wind_row_in,
    wind_col_out,
    wind_col_in,
    row_out,
    row_in,
    col_out,
    col_in,
    coef,
    state_a,
    state_b,
    spread,
    flags,
    band_send,
    band_recv,
    wind_send,
    wind_recv,
    halo_send,
    halo_recv,
):
    bins, nz, rd, cd = conc.shape
    ln, columns = nwp.shape[1:]
    cap = pick.shape[3]
    slots = n_rows * cap
    r = lax.axis_index("rows")
    c = lax.axis_index("cols")
    has = (r > 0, r < n_rows - 1, c > 0, c < n_cols - 1)
    target = ({"rows": r - 1}, {"rows": r + 1}, {"cols": c - 1}, {"cols": c + 1})
    lane = lax.broadcasted_iota(jnp.int32, (rd, cd), 1)
    sub = lax.broadcasted_iota(jnp.int32, (rd, cd), 0)
    odd = (lane % 2) == 1
    first_lane, last_lane = lane == 0, lane == cd - 1
    first_sub, last_sub = sub == 0, sub == rd - 1

    barrier = pltpu.get_barrier_semaphore()
    for d in range(1, n_rows):
        pl.semaphore_signal(
            barrier, inc=1, device_id={"rows": lax.rem(r + d, n_rows)}, device_id_type=MESH
        )
    for side in (LEFT, RIGHT):

        @pl.when(has[side])
        def _():
            pl.semaphore_signal(barrier, inc=1, device_id=target[side], device_id_type=MESH)

    for side in (UP, DOWN):

        @pl.when(jnp.logical_not(has[side]))
        def _():
            row_in[:, side] = jnp.zeros(row_in.shape[:1] + row_in.shape[2:], BF16)
            wind_row_in[side] = jnp.zeros(wind_row_in.shape[1:], BF16)

    for side in (LEFT, RIGHT):

        @pl.when(jnp.logical_not(has[side]))
        def _():
            col_in[:, side - 2] = jnp.zeros(col_in.shape[:1] + col_in.shape[2:], F32)
            wind_col_in[side - 2] = jnp.zeros(wind_col_in.shape[1:], F32)

    groups = nz // rd
    here = [(lane // 2) == g for g in range(groups)]

    def block(g):
        return slice(g * rd, (g + 1) * rd)

    def pack(rows):
        packed = jnp.zeros((rd, cd), F32)
        for y in range(rd):
            acc = jnp.zeros((rd, cd), F32)
            for g in range(groups):
                acc = jnp.where(here[g], pltpu.roll(rows[y][g], 2 * g + 1, 1), acc)
            packed = packed + (pltpu.roll(acc, 2 * groups * y, 1) if y else acc)
        return packed

    def unpack(left, right):
        return jnp.where(odd, pltpu.roll(left, 1, 1), pltpu.roll(right, cd - 1, 1))

    def halo_copy(stage, side, b):
        other = side ^ 1
        if side < 2:
            src, dst = row_out.at[stage, side, b], row_in.at[stage, other, b]
        else:
            src, dst = col_out.at[stage, b], col_in.at[stage, other - 2, b]
        return pltpu.make_async_remote_copy(
            src_ref=src,
            dst_ref=dst,
            send_sem=halo_send.at[stage, side, b],
            recv_sem=halo_recv.at[stage, other, b],
            device_id=target[side],
            device_id_type=MESH,
        )

    def halo_arrival(stage, side, b):
        if side < 2:
            src, dst = row_out.at[stage, side, b], row_in.at[stage, side, b]
        else:
            src, dst = col_out.at[stage, b], col_in.at[stage, side - 2, b]
        return pltpu.make_async_remote_copy(
            src_ref=src,
            dst_ref=dst,
            send_sem=halo_send.at[stage, side, b],
            recv_sem=halo_recv.at[stage, side, b],
            device_id=target[side],
            device_id_type=MESH,
        )

    def wind_copy(side):
        other = side ^ 1
        if side < 2:
            src, dst = wind_row_out.at[side], wind_row_in.at[other]
        else:
            src, dst = wind_col_out, wind_col_in.at[other - 2]
        return pltpu.make_async_remote_copy(
            src_ref=src,
            dst_ref=dst,
            send_sem=wind_send.at[side],
            recv_sem=wind_recv.at[other],
            device_id=target[side],
            device_id_type=MESH,
        )

    def wind_arrival(side):
        if side < 2:
            src, dst = wind_row_out.at[side], wind_row_in.at[side]
        else:
            src, dst = wind_col_out, wind_col_in.at[side - 2]
        return pltpu.make_async_remote_copy(
            src_ref=src,
            dst_ref=dst,
            send_sem=wind_send.at[side],
            recv_sem=wind_recv.at[side],
            device_id=target[side],
            device_id_type=MESH,
        )

    def send_halo(stage, b):
        for side in range(4):

            @pl.when(has[side])
            def _():
                halo_copy(stage, side, b).start()

    flat_conc = conc.reshape(bins * nz * rd, cd)

    def first_pack(b, _):
        rows = []
        for y in range(rd):
            row = flat_conc[pl.ds(b * (nz * rd) + y, nz, stride=rd), :]
            state_a[b, y] = row
            rows.append([row[block(g)] for g in range(groups)])
            if y == 0:
                row_out[0, UP, b] = row.astype(BF16)
            if y == rd - 1:
                row_out[0, DOWN, b] = row.astype(BF16)
        col_out[0, b] = pack(rows)
        return 0

    lax.fori_loop(0, bins, first_pack, 0)

    pl.semaphore_wait(
        barrier, n_rows - 1 + has[LEFT].astype(jnp.int32) + has[RIGHT].astype(jnp.int32)
    )

    def first_send(b, _):
        send_halo(0, b)
        return 0

    lax.fori_loop(0, bins, first_send, 0)

    diag = lax.broadcasted_iota(jnp.int32, (nz, nz), 0) == lax.broadcasted_iota(
        jnp.int32, (nz, nz), 1
    )
    low = jnp.sum(
        jnp.where(diag, lev_lo[...].astype(F32), 0.0), axis=1, keepdims=True
    ).astype(jnp.int32)
    share = jnp.sum(jnp.where(diag, frac[...], 0.0), axis=1, keepdims=True)
    level_id = lax.broadcasted_iota(jnp.int32, (nz, ln), 1)
    interp = jnp.where(level_id == low, 1.0 - share, 0.0) + jnp.where(
        level_id == low + 1, share, 0.0
    )
    interp_hi = interp.astype(BF16)
    rest = interp - interp_hi.astype(F32)
    parts = jnp.concatenate([interp_hi, rest.astype(BF16)], axis=0)
    for f in range(2):
        mixed = jnp.dot(parts, nwp[f], preferred_element_type=F32)
        levels[f * nz : (f + 1) * nz, :] = (mixed[:nz] + mixed[nz:]).astype(BF16)

    def band_copy(source, dest, d):
        return pltpu.make_async_remote_copy(
            src_ref=sent.at[pl.ds(pl.multiple_of(dest * cap, cap), cap)],
            dst_ref=got.at[pl.ds(pl.multiple_of(source * cap, cap), cap)],
            send_sem=band_send.at[d],
            recv_sem=band_recv.at[d],
            device_id={"rows": dest},
            device_id_type=MESH,
        )

    per = 4
    width = per * cap

    def choose(p, _):
        wanted = jnp.concatenate([pick[0, 0, pl.ds(p * per + i, 1), :] for i in range(per)], axis=1)
        step = 128

        def fill(t, _):
            ids = lax.broadcasted_iota(jnp.int32, (step, width), 0) + t * step
            onehot[pl.ds(t * step, step), :] = jnp.where(ids == wanted, 1.0, 0.0).astype(BF16)
            return 0

        lax.fori_loop(0, columns // step, fill, 0)
        chosen = jnp.dot(levels[...], onehot[...], preferred_element_type=F32)
        chosen = jnp.concatenate([chosen, jnp.zeros((128 - 2 * nz, width), F32)], axis=0)
        sent[pl.ds(p * width, width), :] = chosen.T.astype(BF16)
        return 0

    lax.fori_loop(0, n_rows // per, choose, 0)
    for d in range(1, n_rows):
        band_copy(r, lax.rem(r + d, n_rows), d).start()

    weights = corner_wt[...]
    norm_wt[...] = weights / (weights[0] + weights[1] + weights[2] + weights[3])
    chunk = 128

    def fill_table(i, _):
        p = i // (slots // chunk)
        t = i % (slots // chunk)
        ids = lax.broadcasted_iota(jnp.int32, (chunk, cd), 0) + t * chunk
        for half in range(2):
            total = jnp.zeros((chunk, cd), F32)
            for q in range(4):
                slot = corner_slot[q, pl.ds(2 * p + half, 1), :]
                wt = norm_wt[q, pl.ds(2 * p + half, 1), :]
                total = total + jnp.where(ids == slot, wt, 0.0)
            hi = total.astype(BF16)
            where = (p, pl.ds(t * chunk, chunk), pl.ds(half * cd, cd))
            table_hi[where] = hi
            table_lo[where] = (total - hi.astype(F32)).astype(BF16)
        return 0

    lax.fori_loop(0, (rd // 2) * (slots // chunk), fill_table, 0)

    diag = lax.broadcasted_iota(jnp.int32, (nz, nz), 0) == lax.broadcasted_iota(
        jnp.int32, (nz, nz), 1
    )
    for b in range(bins):
        column = jnp.sum(jnp.where(diag, profile[b : b + 1, :], 0.0), axis=1, keepdims=True)
        spread[b] = jnp.broadcast_to(column, (nz, cd))
    flags[...] = source_mask[...].astype(F32)

    own = pl.ds(pl.multiple_of(r * cap, cap), cap)
    got[own, :] = sent[own, :]
    for d in range(1, n_rows):
        band_copy(lax.rem(r + n_rows - d, n_rows), r, d).wait_recv()
    for t in range(slots // 128):
        turned[:, t * 128 : (t + 1) * 128] = (
            got[t * 128 : (t + 1) * 128, :].astype(F32).T.astype(BF16)
        )
    for p in range(rd // 2):
        blown = jnp.dot(turned[...], table_hi[p], preferred_element_type=F32) + jnp.dot(
            turned[...], table_lo[p], preferred_element_type=F32
        )
        winds[2 * p] = blown[: 2 * nz, :cd]
        winds[2 * p + 1] = blown[: 2 * nz, cd:]

    wind_row_out[UP] = winds[0, nz:, :].astype(BF16)
    wind_row_out[DOWN] = winds[rd - 1, nz:, :].astype(BF16)
    wind_col_out[...] = pack([[winds[y, block(g), :] for g in range(groups)] for y in range(rd)])
    for side in range(4):

        @pl.when(has[side])
        def _():
            wind_copy(side).start()

    def wind_wait(sides):
        for side in sides:

            @pl.when(has[side])
            def _():
                wind_arrival(side).wait_recv()

    def across(plane, rim, y, g):
        rim = pltpu.roll(rim, cd - 2 * (y * groups + g) - 1, 1)
        ahead = jnp.where(last_lane, rim, pltpu.roll(plane, cd - 1, 1))
        behind = jnp.where(first_lane, rim, pltpu.roll(plane, 1, 1))
        return ahead, behind

    wind_wait((LEFT, RIGHT))
    wind_rim = unpack(wind_col_in[0], wind_col_in[1])

    def north_row(y):
        if y < 0:
            return wind_row_in[UP].astype(F32)
        return winds[y, nz:, :] if y < rd else wind_row_in[DOWN].astype(F32)

    for y in [*range(1, rd - 1), 0, rd - 1]:
        if y == 0:
            wind_wait((UP, DOWN))
        near = [north_row(y + i) for i in (-1, 0, 1)]
        for g in range(groups):
            k = block(g)
            u = winds[y, k, :]
            u_ahead, u_behind = across(u, wind_rim, y, g)
            v_above, v, v_below = (row[k] for row in near)
            right, left = 0.5 * (u + u_ahead), 0.5 * (u + u_behind)
            down, up = 0.5 * (v + v_below), 0.5 * (v + v_above)
            coef[0, y, k, :] = (
                (1.0 - 4.0 * KAPPA)
                - jnp.maximum(right, 0.0)
                + jnp.minimum(left, 0.0)
                - jnp.maximum(down, 0.0)
                + jnp.minimum(up, 0.0)
            )
            coef[1, y, k, :] = KAPPA - jnp.minimum(right, 0.0)
            coef[2, y, k, :] = KAPPA + jnp.maximum(left, 0.0)
            coef[3, y, k, :] = KAPPA - jnp.minimum(down, 0.0)
            coef[4, y, k, :] = KAPPA + jnp.maximum(up, 0.0)

    flat_out = out.reshape(bins * nz * rd, cd)
    for stage in range(STEPS):
        src = (state_a, state_b)[stage % 2]
        dst = (state_b, state_a)[stage % 2]
        last = stage == STEPS - 1

        def one_bin(b, _):
            for side in range(4):

                @pl.when(has[side])
                def _():
                    halo_arrival(stage, side, b).wait_recv()

            rim = unpack(col_in[stage, 0, b], col_in[stage, 1, b])
            sink = settle[b]
            rows = (
                [row_in[stage, UP, b].astype(F32)]
                + [src[b, y] for y in range(rd)]
                + [row_in[stage, DOWN, b].astype(F32)]
            )
            fresh = []
            for y in range(rd):
                flag = flags[y : y + 1, :]
                news = []
                turned_over = jnp.zeros((rd, cd), F32)
                for g in range(groups):
                    k = block(g)
                    above, a, below = (rows[y + i][k] for i in range(3))
                    ahead, behind = across(a, rim, y, g)
                    falling = sink * a
                    rolled = pltpu.roll(falling, 1, 0)
                    arriving = jnp.where(first_sub, turned_over, rolled)
                    turned_over = rolled
                    new = (
                        (coef[0, y, k, :] * a + coef[1, y, k, :] * ahead)
                        + (coef[2, y, k, :] * behind + coef[3, y, k, :] * below)
                        + (coef[4, y, k, :] * above + flag * spread[b, k, :])
                        + (arriving - falling)
                    )
                    if last:
                        flat_out[pl.ds(b * (nz * rd) + g * (rd * rd) + y, rd, stride=rd), :] = new
                    else:
                        dst[b, y, k, :] = new
                    news.append(new)
                fallen = falling[rd - 1 :, :]
                here_row = (b, slice(y, y + 1), slice(None))
                deposit[here_row] = fallen if stage == 0 else deposit[here_row] + fallen
                fresh.append(news)
                if not last and y == 0:
                    row_out[stage + 1, UP, b] = jnp.concatenate(news, axis=0).astype(BF16)
            if not last:
                row_out[stage + 1, DOWN, b] = jnp.concatenate(fresh[-1], axis=0).astype(BF16)
                col_out[stage + 1, b] = pack(fresh)
                send_halo(stage + 1, b)
            return 0

        lax.fori_loop(0, bins, one_bin, 0)

    for d in range(1, n_rows):
        band_copy(r, lax.rem(r + d, n_rows), d).wait_send()
    for side in range(4):

        @pl.when(has[side])
        def _():
            wind_copy(side).wait_send()

            def drain(b, _):
                for stage in range(STEPS):
                    halo_copy(stage, side, b).wait_send()
                return 0

            lax.fori_loop(0, bins, drain, 0)


def per_device(conc, nwp, lev_lo, frac, pick, corner_slot, corner_wt, settle, source_mask, profile):
    n_rows, n_cols = lax.axis_size("rows"), lax.axis_size("cols")
    bins, nz, rd, cd = conc.shape
    cap = pick.shape[3]
    slots = n_rows * cap
    columns = nwp.shape[2]
    vmem = pl.BlockSpec(memory_space=pltpu.VMEM)
    smem = pl.BlockSpec(memory_space=pltpu.SMEM)
    return pl.pallas_call(
        functools.partial(kernel, n_rows, n_cols),
        out_shape=(
            jax.ShapeDtypeStruct(conc.shape, F32),
            jax.ShapeDtypeStruct((bins, rd, cd), F32),
        ),
        in_specs=[vmem] * 7 + [smem, vmem, vmem],
        out_specs=(vmem, vmem),
        scratch_shapes=[
            pltpu.VMEM((2 * nz, columns), BF16),
            pltpu.VMEM((columns, 4 * cap), BF16),
            pltpu.VMEM((slots, 128), BF16),
            pltpu.VMEM((slots, 128), BF16),
            pltpu.VMEM((128, slots), BF16),
            pltpu.VMEM(corner_wt.shape, F32),
            pltpu.VMEM((rd // 2, slots, 2 * cd), BF16),
            pltpu.VMEM((rd // 2, slots, 2 * cd), BF16),
            pltpu.VMEM((rd, 2 * nz, cd), F32),
            pltpu.VMEM((2, nz, cd), BF16),
            pltpu.VMEM((2, nz, cd), BF16),
            pltpu.VMEM((rd, cd), F32),
            pltpu.VMEM((2, rd, cd), F32),
            pltpu.VMEM((STEPS, 2, bins, nz, cd), BF16),
            pltpu.VMEM((STEPS, 2, bins, nz, cd), BF16),
            pltpu.VMEM((STEPS, bins, rd, cd), F32),
            pltpu.VMEM((STEPS, 2, bins, rd, cd), F32),
            pltpu.VMEM((5, rd, nz, cd), F32),
            pltpu.VMEM((bins, rd, nz, cd), F32),
            pltpu.VMEM((bins, rd, nz, cd), F32),
            pltpu.VMEM((bins, nz, cd), F32),
            pltpu.VMEM((rd, cd), F32),
            pltpu.SemaphoreType.DMA((n_rows,)),
            pltpu.SemaphoreType.DMA((n_rows,)),
            pltpu.SemaphoreType.DMA((4,)),
            pltpu.SemaphoreType.DMA((4,)),
            pltpu.SemaphoreType.DMA((STEPS, 4, bins)),
            pltpu.SemaphoreType.DMA((STEPS, 4, bins)),
        ],
        compiler_params=pltpu.CompilerParams(
            collective_id=0, has_side_effects=True, vmem_limit_bytes=48 * 1024 * 1024
        ),
        cost_estimate=pl.CostEstimate(
            flops=10**9, bytes_accessed=6 * 10**6, transcendentals=0
        ),
        name="ash",
    )(
        conc,
        nwp,
        lev_lo.reshape(1, -1),
        frac.reshape(1, -1),
        pick,
        corner_slot,
        corner_wt,
        settle,
        source_mask,
        profile,
    )


def solution(mesh):
    placed = (
        P(None, None, "rows", "cols"),
        P(None, None, "rows"),
        P(),
        P(),
        P("rows", "cols", None, None),
        P(None, "rows", "cols"),
        P(None, "rows", "cols"),
        P(),
        P("rows", "cols"),
        P(),
    )
    return jax.shard_map(
        per_device,
        mesh=mesh,
        in_specs=placed,
        out_specs=(P(None, None, "rows", "cols"), P(None, "rows", "cols")),
        check_vma=False,
    )
```

```python
import functools

import jax
import jax.numpy as jnp
from jax import lax
from jax.experimental import pallas as pl
from jax.experimental.pallas import tpu as pltpu
from jax.sharding import PartitionSpec as P

STEPS = 3
KAPPA = 0.05
SPAN = 4
MESH = pl.DeviceIdType.MESH
UP, DOWN, LEFT, RIGHT = range(4)
BF16 = jnp.bfloat16
F32 = jnp.float32


def kernel(
    n_rows,
    n_cols,
    conc,
    nwp,
    lev_lo,
    frac,
    pick,
    corner_slot,
    corner_wt,
    settle,
    source_mask,
    profile,
    out,
    deposit,
    levels,
    onehot,
    sent,
    got,
    turned,
    norm_wt,
    table_hi,
    table_lo,
    winds,
    wind_row_out,
    wind_row_in,
    wind_col_out,
    wind_col_in,
    row_out,
    row_in,
    col_out,
    col_in,
    coef,
    state_a,
    state_b,
    spread,
    flags,
    band_send,
    band_recv,
    wind_send,
    wind_recv,
    halo_send,
    halo_recv,
):
    bins, nz, rd, cd = conc.shape
    ln, columns = nwp.shape[1:]
    cap = pick.shape[3]
    slots = n_rows * cap
    r = lax.axis_index("rows")
    c = lax.axis_index("cols")
    has = (r > 0, r < n_rows - 1, c > 0, c < n_cols - 1)
    target = ({"rows": r - 1}, {"rows": r + 1}, {"cols": c - 1}, {"cols": c + 1})
    lane = lax.broadcasted_iota(jnp.int32, (rd, cd), 1)
    sub = lax.broadcasted_iota(jnp.int32, (rd, cd), 0)
    odd = (lane % 2) == 1
    first_lane, last_lane = lane == 0, lane == cd - 1
    first_sub, last_sub = sub == 0, sub == rd - 1

    barrier = pltpu.get_barrier_semaphore()
    for d in range(1, n_rows):
        pl.semaphore_signal(
            barrier, inc=1, device_id={"rows": lax.rem(r + d, n_rows)}, device_id_type=MESH
        )
    for side in (LEFT, RIGHT):

        @pl.when(has[side])
        def _():
            pl.semaphore_signal(barrier, inc=1, device_id=target[side], device_id_type=MESH)

    for side in (UP, DOWN):

        @pl.when(jnp.logical_not(has[side]))
        def _():
            row_in[:, side] = jnp.zeros(row_in.shape[:1] + row_in.shape[2:], BF16)
            wind_row_in[side] = jnp.zeros(wind_row_in.shape[1:], BF16)

    for side in (LEFT, RIGHT):

        @pl.when(jnp.logical_not(has[side]))
        def _():
            col_in[:, side - 2] = jnp.zeros(col_in.shape[:1] + col_in.shape[2:], F32)
            wind_col_in[side - 2] = jnp.zeros(wind_col_in.shape[1:], F32)

    groups = nz // rd
    here = [(lane // 2) == g for g in range(groups)]

    def block(g):
        return slice(g * rd, (g + 1) * rd)

    def pack(rows):
        packed = jnp.zeros((rd, cd), F32)
        for y in range(rd):
            acc = jnp.zeros((rd, cd), F32)
            for g in range(groups):
                acc = jnp.where(here[g], pltpu.roll(rows[y][g], 2 * g + 1, 1), acc)
            packed = packed + (pltpu.roll(acc, 2 * groups * y, 1) if y else acc)
        return packed

    def unpack(left, right):
        return jnp.where(odd, pltpu.roll(left, 1, 1), pltpu.roll(right, cd - 1, 1))

    def halo_copy(stage, side, b, size):
        other = side ^ 1
        some = pl.ds(b, size)
        if side < 2:
            src, dst = row_out.at[stage, side, some], row_in.at[stage, other, some]
        else:
            src, dst = col_out.at[stage, some], col_in.at[stage, other - 2, some]
        return pltpu.make_async_remote_copy(
            src_ref=src,
            dst_ref=dst,
            send_sem=halo_send.at[stage, side, b],
            recv_sem=halo_recv.at[stage, other, b],
            device_id=target[side],
            device_id_type=MESH,
        )

    def halo_arrival(stage, side, b, size):
        some = pl.ds(b, size)
        if side < 2:
            src, dst = row_out.at[stage, side, some], row_in.at[stage, side, some]
        else:
            src, dst = col_out.at[stage, some], col_in.at[stage, side - 2, some]
        return pltpu.make_async_remote_copy(
            src_ref=src,
            dst_ref=dst,
            send_sem=halo_send.at[stage, side, b],
            recv_sem=halo_recv.at[stage, side, b],
            device_id=target[side],
            device_id_type=MESH,
        )

    def wind_copy(side):
        other = side ^ 1
        if side < 2:
            src, dst = wind_row_out.at[side], wind_row_in.at[other]
        else:
            src, dst = wind_col_out, wind_col_in.at[other - 2]
        return pltpu.make_async_remote_copy(
            src_ref=src,
            dst_ref=dst,
            send_sem=wind_send.at[side],
            recv_sem=wind_recv.at[other],
            device_id=target[side],
            device_id_type=MESH,
        )

    def wind_arrival(side):
        if side < 2:
            src, dst = wind_row_out.at[side], wind_row_in.at[side]
        else:
            src, dst = wind_col_out, wind_col_in.at[side - 2]
        return pltpu.make_async_remote_copy(
            src_ref=src,
            dst_ref=dst,
            send_sem=wind_send.at[side],
            recv_sem=wind_recv.at[side],
            device_id=target[side],
            device_id_type=MESH,
        )

    def send_halo(stage, b, size):
        for side in range(4):

            @pl.when(has[side])
            def _():
                halo_copy(stage, side, b, size).start()

    flat_conc = conc.reshape(bins * nz * rd, cd)

    def first_pack(b, _):
        rows = []
        for y in range(rd):
            row = flat_conc[pl.ds(b * (nz * rd) + y, nz, stride=rd), :]
            state_a[b, y] = row
            rows.append([row[block(g)] for g in range(groups)])
            if y == 0:
                row_out[0, UP, b] = row.astype(BF16)
            if y == rd - 1:
                row_out[0, DOWN, b] = row.astype(BF16)
        col_out[0, b] = pack(rows)
        return 0

    lax.fori_loop(0, bins, first_pack, 0)

    diag = lax.broadcasted_iota(jnp.int32, (nz, nz), 0) == lax.broadcasted_iota(
        jnp.int32, (nz, nz), 1
    )
    low = jnp.sum(
        jnp.where(diag, lev_lo[...].astype(F32), 0.0), axis=1, keepdims=True
    ).astype(jnp.int32)
    share = jnp.sum(jnp.where(diag, frac[...], 0.0), axis=1, keepdims=True)
    level_id = lax.broadcasted_iota(jnp.int32, (nz, ln), 1)
    interp = jnp.where(level_id == low, 1.0 - share, 0.0) + jnp.where(
        level_id == low + 1, share, 0.0
    )
    interp_hi = interp.astype(BF16)
    rest = interp - interp_hi.astype(F32)
    parts = jnp.concatenate([interp_hi, rest.astype(BF16)], axis=0)
    for f in range(2):
        mixed = jnp.dot(parts, nwp[f], preferred_element_type=F32)
        levels[f * nz : (f + 1) * nz, :] = (mixed[:nz] + mixed[nz:]).astype(BF16)

    def band_copy(source, dest, d):
        return pltpu.make_async_remote_copy(
            src_ref=sent.at[pl.ds(pl.multiple_of(dest * cap, cap), cap)],
            dst_ref=got.at[pl.ds(pl.multiple_of(source * cap, cap), cap)],
            send_sem=band_send.at[d],
            recv_sem=band_recv.at[d],
            device_id={"rows": dest},
            device_id_type=MESH,
        )

    per = 4
    width = per * cap

    def choose(p, _):
        wanted = jnp.concatenate([pick[0, 0, pl.ds(p * per + i, 1), :] for i in range(per)], axis=1)
        step = 128

        def fill(t, _):
            ids = lax.broadcasted_iota(jnp.int32, (step, width), 0) + t * step
            onehot[pl.ds(t * step, step), :] = jnp.where(ids == wanted, 1.0, 0.0).astype(BF16)
            return 0

        lax.fori_loop(0, columns // step, fill, 0)
        chosen = jnp.dot(levels[...], onehot[...], preferred_element_type=F32)
        chosen = jnp.concatenate([chosen, jnp.zeros((128 - 2 * nz, width), F32)], axis=0)
        sent[pl.ds(p * width, width), :] = chosen.T.astype(BF16)
        return 0

    lax.fori_loop(0, n_rows // per, choose, 0)

    pl.semaphore_wait(
        barrier, n_rows - 1 + has[LEFT].astype(jnp.int32) + has[RIGHT].astype(jnp.int32)
    )
    for d in range(1, n_rows):
        band_copy(r, lax.rem(r + d, n_rows), d).start()
    send_halo(0, 0, bins)

    weights = corner_wt[...]
    norm_wt[...] = weights / (weights[0] + weights[1] + weights[2] + weights[3])
    chunk = 128

    def fill_table(i, _):
        p = i // (slots // chunk)
        t = i % (slots // chunk)
        ids = lax.broadcasted_iota(jnp.int32, (chunk, cd), 0) + t * chunk
        for half in range(2):
            total = jnp.zeros((chunk, cd), F32)
            for q in range(4):
                slot = corner_slot[q, pl.ds(2 * p + half, 1), :]
                wt = norm_wt[q, pl.ds(2 * p + half, 1), :]
                total = total + jnp.where(ids == slot, wt, 0.0)
            hi = total.astype(BF16)
            where = (p, pl.ds(t * chunk, chunk), pl.ds(half * cd, cd))
            table_hi[where] = hi
            table_lo[where] = (total - hi.astype(F32)).astype(BF16)
        return 0

    lax.fori_loop(0, (rd // 2) * (slots // chunk), fill_table, 0)

    diag = lax.broadcasted_iota(jnp.int32, (nz, nz), 0) == lax.broadcasted_iota(
        jnp.int32, (nz, nz), 1
    )
    for b in range(bins):
        column = jnp.sum(jnp.where(diag, profile[b : b + 1, :], 0.0), axis=1, keepdims=True)
        spread[b] = jnp.broadcast_to(column, (nz, cd))
    flags[...] = source_mask[...].astype(F32)

    own = pl.ds(pl.multiple_of(r * cap, cap), cap)
    got[own, :] = sent[own, :]
    for d in range(1, n_rows):
        band_copy(lax.rem(r + n_rows - d, n_rows), r, d).wait_recv()
    for t in range(slots // 128):
        turned[:, t * 128 : (t + 1) * 128] = (
            got[t * 128 : (t + 1) * 128, :].astype(F32).T.astype(BF16)
        )
    for p in range(rd // 2):
        blown = jnp.dot(turned[...], table_hi[p], preferred_element_type=F32) + jnp.dot(
            turned[...], table_lo[p], preferred_element_type=F32
        )
        winds[2 * p] = blown[: 2 * nz, :cd]
        winds[2 * p + 1] = blown[: 2 * nz, cd:]

    wind_row_out[UP] = winds[0, nz:, :].astype(BF16)
    wind_row_out[DOWN] = winds[rd - 1, nz:, :].astype(BF16)
    wind_col_out[...] = pack([[winds[y, block(g), :] for g in range(groups)] for y in range(rd)])
    for side in range(4):

        @pl.when(has[side])
        def _():
            wind_copy(side).start()

    def wind_wait(sides):
        for side in sides:

            @pl.when(has[side])
            def _():
                wind_arrival(side).wait_recv()

    def across(plane, rim, y, g):
        rim = pltpu.roll(rim, cd - 2 * (y * groups + g) - 1, 1)
        ahead = jnp.where(last_lane, rim, pltpu.roll(plane, cd - 1, 1))
        behind = jnp.where(first_lane, rim, pltpu.roll(plane, 1, 1))
        return ahead, behind

    wind_wait((LEFT, RIGHT))
    wind_rim = unpack(wind_col_in[0], wind_col_in[1])

    def north_row(y):
        if y < 0:
            return wind_row_in[UP].astype(F32)
        return winds[y, nz:, :] if y < rd else wind_row_in[DOWN].astype(F32)

    for y in [*range(1, rd - 1), 0, rd - 1]:
        if y == 0:
            wind_wait((UP, DOWN))
        near = [north_row(y + i) for i in (-1, 0, 1)]
        for g in range(groups):
            k = block(g)
            u = winds[y, k, :]
            u_ahead, u_behind = across(u, wind_rim, y, g)
            v_above, v, v_below = (row[k] for row in near)
            right, left = 0.5 * (u + u_ahead), 0.5 * (u + u_behind)
            down, up = 0.5 * (v + v_below), 0.5 * (v + v_above)
            coef[0, y, k, :] = (
                (1.0 - 4.0 * KAPPA)
                - jnp.maximum(right, 0.0)
                + jnp.minimum(left, 0.0)
                - jnp.maximum(down, 0.0)
                + jnp.minimum(up, 0.0)
            )
            coef[1, y, k, :] = KAPPA - jnp.minimum(right, 0.0)
            coef[2, y, k, :] = KAPPA + jnp.maximum(left, 0.0)
            coef[3, y, k, :] = KAPPA - jnp.minimum(down, 0.0)
            coef[4, y, k, :] = KAPPA + jnp.maximum(up, 0.0)

    flat_out = out.reshape(bins * nz * rd, cd)
    for stage in range(STEPS):
        src = (state_a, state_b)[stage % 2]
        dst = (state_b, state_a)[stage % 2]
        last = stage == STEPS - 1

        def one_bin(b, _):
            rim = unpack(col_in[stage, 0, b], col_in[stage, 1, b])
            sink = settle[b]
            rows = (
                [row_in[stage, UP, b].astype(F32)]
                + [src[b, y] for y in range(rd)]
                + [row_in[stage, DOWN, b].astype(F32)]
            )
            fresh = []
            for y in range(rd):
                flag = flags[y : y + 1, :]
                news = []
                turned_over = jnp.zeros((rd, cd), F32)
                for g in range(groups):
                    k = block(g)
                    above, a, below = (rows[y + i][k] for i in range(3))
                    ahead, behind = across(a, rim, y, g)
                    falling = sink * a
                    rolled = pltpu.roll(falling, 1, 0)
                    arriving = jnp.where(first_sub, turned_over, rolled)
                    turned_over = rolled
                    new = (
                        (coef[0, y, k, :] * a + coef[1, y, k, :] * ahead)
                        + (coef[2, y, k, :] * behind + coef[3, y, k, :] * below)
                        + (coef[4, y, k, :] * above + flag * spread[b, k, :])
                        + (arriving - falling)
                    )
                    if last:
                        flat_out[pl.ds(b * (nz * rd) + g * (rd * rd) + y, rd, stride=rd), :] = new
                    else:
                        dst[b, y, k, :] = new
                    news.append(new)
                fallen = falling[rd - 1 :, :]
                here_row = (b, slice(y, y + 1), slice(None))
                deposit[here_row] = fallen if stage == 0 else deposit[here_row] + fallen
                fresh.append(news)
                if not last and y == 0:
                    row_out[stage + 1, UP, b] = jnp.concatenate(news, axis=0).astype(BF16)
            if not last:
                row_out[stage + 1, DOWN, b] = jnp.concatenate(fresh[-1], axis=0).astype(BF16)
                col_out[stage + 1, b] = pack(fresh)
            return 0

        size = bins if stage == 0 else SPAN

        def one_span(i, _):
            for side in range(4):

                @pl.when(has[side])
                def _():
                    halo_arrival(stage, side, i * size, size).wait_recv()

            def one_part(j, _):
                first = i * size + j * SPAN
                lax.fori_loop(first, first + SPAN, one_bin, 0)
                if not last:
                    send_halo(stage + 1, first, SPAN)
                return 0

            return lax.fori_loop(0, size // SPAN, one_part, 0)

        lax.fori_loop(0, bins // size, one_span, 0)

    for d in range(1, n_rows):
        band_copy(r, lax.rem(r + d, n_rows), d).wait_send()
    for side in range(4):

        @pl.when(has[side])
        def _():
            wind_copy(side).wait_send()

            halo_copy(0, side, 0, bins).wait_send()
            for stage in range(1, STEPS):
                for b in range(0, bins, SPAN):
                    halo_copy(stage, side, b, SPAN).wait_send()


def per_device(conc, nwp, lev_lo, frac, pick, corner_slot, corner_wt, settle, source_mask, profile):
    n_rows, n_cols = lax.axis_size("rows"), lax.axis_size("cols")
    bins, nz, rd, cd = conc.shape
    cap = pick.shape[3]
    slots = n_rows * cap
    columns = nwp.shape[2]
    vmem = pl.BlockSpec(memory_space=pltpu.VMEM)
    smem = pl.BlockSpec(memory_space=pltpu.SMEM)
    return pl.pallas_call(
        functools.partial(kernel, n_rows, n_cols),
        out_shape=(
            jax.ShapeDtypeStruct(conc.shape, F32),
            jax.ShapeDtypeStruct((bins, rd, cd), F32),
        ),
        in_specs=[vmem] * 7 + [smem, vmem, vmem],
        out_specs=(vmem, vmem),
        scratch_shapes=[
            pltpu.VMEM((2 * nz, columns), BF16),
            pltpu.VMEM((columns, 4 * cap), BF16),
            pltpu.VMEM((slots, 128), BF16),
            pltpu.VMEM((slots, 128), BF16),
            pltpu.VMEM((128, slots), BF16),
            pltpu.VMEM(corner_wt.shape, F32),
            pltpu.VMEM((rd // 2, slots, 2 * cd), BF16),
            pltpu.VMEM((rd // 2, slots, 2 * cd), BF16),
            pltpu.VMEM((rd, 2 * nz, cd), F32),
            pltpu.VMEM((2, nz, cd), BF16),
            pltpu.VMEM((2, nz, cd), BF16),
            pltpu.VMEM((rd, cd), F32),
            pltpu.VMEM((2, rd, cd), F32),
            pltpu.VMEM((STEPS, 2, bins, nz, cd), BF16),
            pltpu.VMEM((STEPS, 2, bins, nz, cd), BF16),
            pltpu.VMEM((STEPS, bins, rd, cd), F32),
            pltpu.VMEM((STEPS, 2, bins, rd, cd), F32),
            pltpu.VMEM((5, rd, nz, cd), F32),
            pltpu.VMEM((bins, rd, nz, cd), F32),
            pltpu.VMEM((bins, rd, nz, cd), F32),
            pltpu.VMEM((bins, nz, cd), F32),
            pltpu.VMEM((rd, cd), F32),
            pltpu.SemaphoreType.DMA((n_rows,)),
            pltpu.SemaphoreType.DMA((n_rows,)),
            pltpu.SemaphoreType.DMA((4,)),
            pltpu.SemaphoreType.DMA((4,)),
            pltpu.SemaphoreType.DMA((STEPS, 4, bins)),
            pltpu.SemaphoreType.DMA((STEPS, 4, bins)),
        ],
        compiler_params=pltpu.CompilerParams(
            collective_id=0, has_side_effects=True, vmem_limit_bytes=48 * 1024 * 1024
        ),
        cost_estimate=pl.CostEstimate(
            flops=10**9, bytes_accessed=6 * 10**6, transcendentals=0
        ),
        name="ash",
    )(
        conc,
        nwp,
        lev_lo.reshape(1, -1),
        frac.reshape(1, -1),
        pick,
        corner_slot,
        corner_wt,
        settle,
        source_mask,
        profile,
    )


def solution(mesh):
    placed = (
        P(None, None, "rows", "cols"),
        P(None, None, "rows"),
        P(),
        P(),
        P("rows", "cols", None, None),
        P(None, "rows", "cols"),
        P(None, "rows", "cols"),
        P(),
        P("rows", "cols"),
        P(),
    )
    return jax.shard_map(
        per_device,
        mesh=mesh,
        in_specs=placed,
        out_specs=(P(None, None, "rows", "cols"), P(None, "rows", "cols")),
        check_vma=False,
    )
```

```python
import functools

import jax
import jax.numpy as jnp
from jax import lax
from jax.experimental import pallas as pl
from jax.experimental.pallas import tpu as pltpu
from jax.sharding import PartitionSpec as P

STEPS = 3
KAPPA = 0.05
MESH = pl.DeviceIdType.MESH
UP, DOWN, LEFT, RIGHT = range(4)
BF16 = jnp.bfloat16
F32 = jnp.float32


def kernel(
    n_rows,
    n_cols,
    conc,
    nwp,
    lev_lo,
    frac,
    pick,
    corner_slot,
    corner_wt,
    settle,
    source_mask,
    profile,
    out,
    deposit,
    levels,
    onehot,
    sent,
    got,
    turned,
    norm_wt,
    table_hi,
    table_lo,
    winds,
    wind_row_out,
    wind_row_in,
    wind_col_out,
    wind_col_in,
    row_out,
    row_in,
    col_out,
    col_in,
    coef,
    state_a,
    state_b,
    spread,
    flags,
    band_send,
    band_recv,
    wind_send,
    wind_recv,
    halo_send,
    halo_recv,
):
    bins, nz, rd, cd = conc.shape
    ln, columns = nwp.shape[1:]
    cap = pick.shape[3]
    slots = n_rows * cap
    r = lax.axis_index("rows")
    c = lax.axis_index("cols")
    has = (r > 0, r < n_rows - 1, c > 0, c < n_cols - 1)
    target = ({"rows": r - 1}, {"rows": r + 1}, {"cols": c - 1}, {"cols": c + 1})
    lane = lax.broadcasted_iota(jnp.int32, (rd, cd), 1)
    sub = lax.broadcasted_iota(jnp.int32, (rd, cd), 0)
    odd = (lane % 2) == 1
    first_lane, last_lane = lane == 0, lane == cd - 1
    first_sub, last_sub = sub == 0, sub == rd - 1

    barrier = pltpu.get_barrier_semaphore()
    for d in range(1, n_rows):
        pl.semaphore_signal(
            barrier, inc=1, device_id={"rows": lax.rem(r + d, n_rows)}, device_id_type=MESH
        )
    for side in (LEFT, RIGHT):

        @pl.when(has[side])
        def _():
            pl.semaphore_signal(barrier, inc=1, device_id=target[side], device_id_type=MESH)

    for side in (UP, DOWN):

        @pl.when(jnp.logical_not(has[side]))
        def _():
            row_in[:, side] = jnp.zeros(row_in.shape[:1] + row_in.shape[2:], BF16)
            wind_row_in[side] = jnp.zeros(wind_row_in.shape[1:], BF16)

    for side in (LEFT, RIGHT):

        @pl.when(jnp.logical_not(has[side]))
        def _():
            col_in[:, side - 2] = jnp.zeros(col_in.shape[:1] + col_in.shape[2:], F32)
            wind_col_in[side - 2] = jnp.zeros(wind_col_in.shape[1:], F32)

    groups = nz // rd
    here = [(lane // 2) == g for g in range(groups)]

    def block(g):
        return slice(g * rd, (g + 1) * rd)

    def pack(rows):
        packed = jnp.zeros((rd, cd), F32)
        for y in range(rd):
            acc = jnp.zeros((rd, cd), F32)
            for g in range(groups):
                acc = jnp.where(here[g], pltpu.roll(rows[y][g], 2 * g + 1, 1), acc)
            packed = packed + (pltpu.roll(acc, 2 * groups * y, 1) if y else acc)
        return packed

    def unpack(left, right):
        return jnp.where(odd, pltpu.roll(left, 1, 1), pltpu.roll(right, cd - 1, 1))

    def halo_copy(stage, side, b):
        other = side ^ 1
        if side < 2:
            src, dst = row_out.at[stage, side, b], row_in.at[stage, other, b]
        else:
            src, dst = col_out.at[stage, b], col_in.at[stage, other - 2, b]
        return pltpu.make_async_remote_copy(
            src_ref=src,
            dst_ref=dst,
            send_sem=halo_send.at[stage, side, b],
            recv_sem=halo_recv.at[stage, other, b],
            device_id=target[side],
            device_id_type=MESH,
        )

    def halo_arrival(stage, side, b):
        if side < 2:
            src, dst = row_out.at[stage, side, b], row_in.at[stage, side, b]
        else:
            src, dst = col_out.at[stage, b], col_in.at[stage, side - 2, b]
        return pltpu.make_async_remote_copy(
            src_ref=src,
            dst_ref=dst,
            send_sem=halo_send.at[stage, side, b],
            recv_sem=halo_recv.at[stage, side, b],
            device_id=target[side],
            device_id_type=MESH,
        )

    def wind_copy(side):
        other = side ^ 1
        if side < 2:
            src, dst = wind_row_out.at[side], wind_row_in.at[other]
        else:
            src, dst = wind_col_out, wind_col_in.at[other - 2]
        return pltpu.make_async_remote_copy(
            src_ref=src,
            dst_ref=dst,
            send_sem=wind_send.at[side],
            recv_sem=wind_recv.at[other],
            device_id=target[side],
            device_id_type=MESH,
        )

    def wind_arrival(side):
        if side < 2:
            src, dst = wind_row_out.at[side], wind_row_in.at[side]
        else:
            src, dst = wind_col_out, wind_col_in.at[side - 2]
        return pltpu.make_async_remote_copy(
            src_ref=src,
            dst_ref=dst,
            send_sem=wind_send.at[side],
            recv_sem=wind_recv.at[side],
            device_id=target[side],
            device_id_type=MESH,
        )

    def send_halo(stage, b):
        for side in range(4):

            @pl.when(has[side])
            def _():
                halo_copy(stage, side, b).start()

    flat_conc = conc.reshape(bins * nz * rd, cd)

    def first_pack(b, _):
        rows = []
        for y in range(rd):
            row = flat_conc[pl.ds(b * (nz * rd) + y, nz, stride=rd), :]
            state_a[b, y] = row
            rows.append([row[block(g)] for g in range(groups)])
            if y == 0:
                row_out[0, UP, b] = row.astype(BF16)
            if y == rd - 1:
                row_out[0, DOWN, b] = row.astype(BF16)
        col_out[0, b] = pack(rows)
        return 0

    lax.fori_loop(0, bins, first_pack, 0)

    diag = lax.broadcasted_iota(jnp.int32, (nz, nz), 0) == lax.broadcasted_iota(
        jnp.int32, (nz, nz), 1
    )
    low = jnp.sum(
        jnp.where(diag, lev_lo[...].astype(F32), 0.0), axis=1, keepdims=True
    ).astype(jnp.int32)
    share = jnp.sum(jnp.where(diag, frac[...], 0.0), axis=1, keepdims=True)
    level_id = lax.broadcasted_iota(jnp.int32, (nz, ln), 1)
    interp = jnp.where(level_id == low, 1.0 - share, 0.0) + jnp.where(
        level_id == low + 1, share, 0.0
    )
    interp_hi = interp.astype(BF16)
    rest = interp - interp_hi.astype(F32)
    parts = jnp.concatenate([interp_hi, rest.astype(BF16)], axis=0)
    for f in range(2):
        mixed = jnp.dot(parts, nwp[f], preferred_element_type=F32)
        levels[f * nz : (f + 1) * nz, :] = (mixed[:nz] + mixed[nz:]).astype(BF16)

    def band_copy(source, dest, d):
        return pltpu.make_async_remote_copy(
            src_ref=sent.at[pl.ds(pl.multiple_of(dest * cap, cap), cap)],
            dst_ref=got.at[pl.ds(pl.multiple_of(source * cap, cap), cap)],
            send_sem=band_send.at[d],
            recv_sem=band_recv.at[d],
            device_id={"rows": dest},
            device_id_type=MESH,
        )

    per = 4
    width = per * cap

    def choose(p, _):
        wanted = jnp.concatenate([pick[0, 0, pl.ds(p * per + i, 1), :] for i in range(per)], axis=1)
        step = 128

        def fill(t, _):
            ids = lax.broadcasted_iota(jnp.int32, (step, width), 0) + t * step
            onehot[pl.ds(t * step, step), :] = jnp.where(ids == wanted, 1.0, 0.0).astype(BF16)
            return 0

        lax.fori_loop(0, columns // step, fill, 0)
        chosen = jnp.dot(levels[...], onehot[...], preferred_element_type=F32)
        chosen = jnp.concatenate([chosen, jnp.zeros((128 - 2 * nz, width), F32)], axis=0)
        sent[pl.ds(p * width, width), :] = chosen.T.astype(BF16)
        return 0

    lax.fori_loop(0, n_rows // per, choose, 0)
    pl.semaphore_wait(
        barrier, n_rows - 1 + has[LEFT].astype(jnp.int32) + has[RIGHT].astype(jnp.int32)
    )
    for d in range(1, n_rows):
        band_copy(r, lax.rem(r + d, n_rows), d).start()

    def first_send(b, _):
        send_halo(0, b)
        return 0

    lax.fori_loop(0, bins, first_send, 0)


    weights = corner_wt[...]
    norm_wt[...] = weights / (weights[0] + weights[1] + weights[2] + weights[3])
    chunk = 128

    def fill_table(i, _):
        p = i // (slots // chunk)
        t = i % (slots // chunk)
        ids = lax.broadcasted_iota(jnp.int32, (chunk, cd), 0) + t * chunk
        for half in range(2):
            total = jnp.zeros((chunk, cd), F32)
            for q in range(4):
                slot = corner_slot[q, pl.ds(2 * p + half, 1), :]
                wt = norm_wt[q, pl.ds(2 * p + half, 1), :]
                total = total + jnp.where(ids == slot, wt, 0.0)
            hi = total.astype(BF16)
            where = (p, pl.ds(t * chunk, chunk), pl.ds(half * cd, cd))
            table_hi[where] = hi
            table_lo[where] = (total - hi.astype(F32)).astype(BF16)
        return 0

    lax.fori_loop(0, (rd // 2) * (slots // chunk), fill_table, 0)

    diag = lax.broadcasted_iota(jnp.int32, (nz, nz), 0) == lax.broadcasted_iota(
        jnp.int32, (nz, nz), 1
    )
    for b in range(bins):
        column = jnp.sum(jnp.where(diag, profile[b : b + 1, :], 0.0), axis=1, keepdims=True)
        spread[b] = jnp.broadcast_to(column, (nz, cd))
    flags[...] = source_mask[...].astype(F32)

    own = pl.ds(pl.multiple_of(r * cap, cap), cap)
    got[own, :] = sent[own, :]
    for d in range(1, n_rows):
        band_copy(lax.rem(r + n_rows - d, n_rows), r, d).wait_recv()
    for t in range(slots // 128):
        turned[:, t * 128 : (t + 1) * 128] = (
            got[t * 128 : (t + 1) * 128, :].astype(F32).T.astype(BF16)
        )
    for p in range(rd // 2):
        blown = jnp.dot(turned[...], table_hi[p], preferred_element_type=F32) + jnp.dot(
            turned[...], table_lo[p], preferred_element_type=F32
        )
        winds[2 * p] = blown[: 2 * nz, :cd]
        winds[2 * p + 1] = blown[: 2 * nz, cd:]

    wind_row_out[UP] = winds[0, nz:, :].astype(BF16)
    wind_row_out[DOWN] = winds[rd - 1, nz:, :].astype(BF16)
    wind_col_out[...] = pack([[winds[y, block(g), :] for g in range(groups)] for y in range(rd)])
    for side in range(4):

        @pl.when(has[side])
        def _():
            wind_copy(side).start()

    def wind_wait(sides):
        for side in sides:

            @pl.when(has[side])
            def _():
                wind_arrival(side).wait_recv()

    def across(plane, rim, y, g):
        rim = pltpu.roll(rim, cd - 2 * (y * groups + g) - 1, 1)
        ahead = jnp.where(last_lane, rim, pltpu.roll(plane, cd - 1, 1))
        behind = jnp.where(first_lane, rim, pltpu.roll(plane, 1, 1))
        return ahead, behind

    wind_wait((LEFT, RIGHT))
    wind_rim = unpack(wind_col_in[0], wind_col_in[1])

    def north_row(y):
        if y < 0:
            return wind_row_in[UP].astype(F32)
        return winds[y, nz:, :] if y < rd else wind_row_in[DOWN].astype(F32)

    for y in [*range(1, rd - 1), 0, rd - 1]:
        if y == 0:
            wind_wait((UP, DOWN))
        near = [north_row(y + i) for i in (-1, 0, 1)]
        for g in range(groups):
            k = block(g)
            u = winds[y, k, :]
            u_ahead, u_behind = across(u, wind_rim, y, g)
            v_above, v, v_below = (row[k] for row in near)
            right, left = 0.5 * (u + u_ahead), 0.5 * (u + u_behind)
            down, up = 0.5 * (v + v_below), 0.5 * (v + v_above)
            coef[0, y, k, :] = (
                (1.0 - 4.0 * KAPPA)
                - jnp.maximum(right, 0.0)
                + jnp.minimum(left, 0.0)
                - jnp.maximum(down, 0.0)
                + jnp.minimum(up, 0.0)
            )
            coef[1, y, k, :] = KAPPA - jnp.minimum(right, 0.0)
            coef[2, y, k, :] = KAPPA + jnp.maximum(left, 0.0)
            coef[3, y, k, :] = KAPPA - jnp.minimum(down, 0.0)
            coef[4, y, k, :] = KAPPA + jnp.maximum(up, 0.0)

    flat_out = out.reshape(bins * nz * rd, cd)
    for stage in range(STEPS):
        src = (state_a, state_b)[stage % 2]
        dst = (state_b, state_a)[stage % 2]
        last = stage == STEPS - 1

        def one_bin(b, _):
            for side in range(4):

                @pl.when(has[side])
                def _():
                    halo_arrival(stage, side, b).wait_recv()
                    halo_copy(stage, side, b).wait_send()

            rim = unpack(col_in[stage, 0, b], col_in[stage, 1, b])
            sink = settle[b]
            rows = (
                [row_in[stage, UP, b].astype(F32)]
                + [src[b, y] for y in range(rd)]
                + [row_in[stage, DOWN, b].astype(F32)]
            )
            fresh = []
            for y in range(rd):
                flag = flags[y : y + 1, :]
                news = []
                turned_over = jnp.zeros((rd, cd), F32)
                for g in range(groups):
                    k = block(g)
                    above, a, below = (rows[y + i][k] for i in range(3))
                    ahead, behind = across(a, rim, y, g)
                    falling = sink * a
                    rolled = pltpu.roll(falling, 1, 0)
                    arriving = jnp.where(first_sub, turned_over, rolled)
                    turned_over = rolled
                    new = (
                        (coef[0, y, k, :] * a + coef[1, y, k, :] * ahead)
                        + (coef[2, y, k, :] * behind + coef[3, y, k, :] * below)
                        + (coef[4, y, k, :] * above + flag * spread[b, k, :])
                        + (arriving - falling)
                    )
                    if last:
                        flat_out[pl.ds(b * (nz * rd) + g * (rd * rd) + y, rd, stride=rd), :] = new
                    else:
                        dst[b, y, k, :] = new
                    news.append(new)
                fallen = falling[rd - 1 :, :]
                here_row = (b, slice(y, y + 1), slice(None))
                deposit[here_row] = fallen if stage == 0 else deposit[here_row] + fallen
                fresh.append(news)
                if not last and y == 0:
                    row_out[stage + 1, UP, b] = jnp.concatenate(news, axis=0).astype(BF16)
            if not last:
                row_out[stage + 1, DOWN, b] = jnp.concatenate(fresh[-1], axis=0).astype(BF16)
                col_out[stage + 1, b] = pack(fresh)
                send_halo(stage + 1, b)
            return 0

        lax.fori_loop(0, bins, one_bin, 0)

    for d in range(1, n_rows):
        band_copy(r, lax.rem(r + d, n_rows), d).wait_send()
    for side in range(4):

        @pl.when(has[side])
        def _():
            wind_copy(side).wait_send()


def per_device(conc, nwp, lev_lo, frac, pick, corner_slot, corner_wt, settle, source_mask, profile):
    n_rows, n_cols = lax.axis_size("rows"), lax.axis_size("cols")
    bins, nz, rd, cd = conc.shape
    cap = pick.shape[3]
    slots = n_rows * cap
    columns = nwp.shape[2]
    vmem = pl.BlockSpec(memory_space=pltpu.VMEM)
    smem = pl.BlockSpec(memory_space=pltpu.SMEM)
    return pl.pallas_call(
        functools.partial(kernel, n_rows, n_cols),
        out_shape=(
            jax.ShapeDtypeStruct(conc.shape, F32),
            jax.ShapeDtypeStruct((bins, rd, cd), F32),
        ),
        in_specs=[vmem] * 7 + [smem, vmem, vmem],
        out_specs=(vmem, vmem),
        scratch_shapes=[
            pltpu.VMEM((2 * nz, columns), BF16),
            pltpu.VMEM((columns, 4 * cap), BF16),
            pltpu.VMEM((slots, 128), BF16),
            pltpu.VMEM((slots, 128), BF16),
            pltpu.VMEM((128, slots), BF16),
            pltpu.VMEM(corner_wt.shape, F32),
            pltpu.VMEM((rd // 2, slots, 2 * cd), BF16),
            pltpu.VMEM((rd // 2, slots, 2 * cd), BF16),
            pltpu.VMEM((rd, 2 * nz, cd), F32),
            pltpu.VMEM((2, nz, cd), BF16),
            pltpu.VMEM((2, nz, cd), BF16),
            pltpu.VMEM((rd, cd), F32),
            pltpu.VMEM((2, rd, cd), F32),
            pltpu.VMEM((STEPS, 2, bins, nz, cd), BF16),
            pltpu.VMEM((STEPS, 2, bins, nz, cd), BF16),
            pltpu.VMEM((STEPS, bins, rd, cd), F32),
            pltpu.VMEM((STEPS, 2, bins, rd, cd), F32),
            pltpu.VMEM((5, rd, nz, cd), F32),
            pltpu.VMEM((bins, rd, nz, cd), F32),
            pltpu.VMEM((bins, rd, nz, cd), F32),
            pltpu.VMEM((bins, nz, cd), F32),
            pltpu.VMEM((rd, cd), F32),
            pltpu.SemaphoreType.DMA((n_rows,)),
            pltpu.SemaphoreType.DMA((n_rows,)),
            pltpu.SemaphoreType.DMA((4,)),
            pltpu.SemaphoreType.DMA((4,)),
            pltpu.SemaphoreType.DMA((STEPS, 4, bins)),
            pltpu.SemaphoreType.DMA((STEPS, 4, bins)),
        ],
        compiler_params=pltpu.CompilerParams(
            collective_id=0, has_side_effects=True, vmem_limit_bytes=48 * 1024 * 1024
        ),
        cost_estimate=pl.CostEstimate(
            flops=10**9, bytes_accessed=6 * 10**6, transcendentals=0
        ),
        name="ash",
    )(
        conc,
        nwp,
        lev_lo.reshape(1, -1),
        frac.reshape(1, -1),
        pick,
        corner_slot,
        corner_wt,
        settle,
        source_mask,
        profile,
    )


def solution(mesh):
    placed = (
        P(None, None, "rows", "cols"),
        P(None, None, "rows"),
        P(),
        P(),
        P("rows", "cols", None, None),
        P(None, "rows", "cols"),
        P(None, "rows", "cols"),
        P(),
        P("rows", "cols"),
        P(),
    )
    return jax.shard_map(
        per_device,
        mesh=mesh,
        in_specs=placed,
        out_specs=(P(None, None, "rows", "cols"), P(None, "rows", "cols")),
        check_vma=False,
    )
```
